128 devices in a mesh: frame: 16 (over z_lo, x, core), mp: 8 (over z_hi, y).
Axes of the slice: x: 4, y: 4, z: 4 (z_hi: 2, z_lo: 2; z = z_hi * 2 + z_lo), core: 2. Of those that a mesh axis runs over, the one named last changes fastest.
Arguments:
- stream: bfloat16 [65536, 1408], P('frame'), may hold values from -6 to 6
- norm_gain: float32 [1408], replicated, may hold values from 0.1 to 1.9
- w_qkv: bfloat16 [3, 1408, 1408], P(None, None, 'mp'), may hold values from -1 to 1
- w_out: bfloat16 [1408, 1408], P('mp'), may hold values from -0.15625 to 0.15625
- pool_gain: float32 [1408], replicated, may hold values from 0.1 to 1.9
- w_llm: bfloat16 [1408, 4096], P(None, 'mp'), may hold values from -0.15625 to 0.15625
- owner_slot: int32 [16384], replicated, may hold values from 0 to 16383, as said below
Outputs:
- llm_rows: bfloat16 [16384, 4096], P('frame', 'mp')
The draws below stay inside these ranges and needn't reach their ends.
Inputs may be any that keep to these rules, and one draw needn't show every extreme that they name: owner_slot is a permutation of the 16384 rows; the pooled rows of each aligned block of 1024 send exactly 64 rows into each aligned block of 1024 destinations.
All inputs are finite; a program needn't handle non-finite values.
Results may differ from the reference program's by a relative error of at most 0.009.
Values may be sent and summed in bfloat16 or wider, within the bound.
A program may use at most 128 MiB of HBM per device.

```python
import jax
import jax.numpy as jnp
from jax import lax

D = 1408
HEADS = 16
HDIM = 88
LLM_D = 4096
FRAMES = 128
PATCHES = 256
CLIPS = 2
TOKENS = 65536
POOLED_DEV = 1024
POOLED = 16384


def draw_stream(key, part):
    key = jax.random.fold_in(key, 1)
    key_base = jax.random.fold_in(key, 0)
    values = jax.random.normal(key_base, (TOKENS, D), jnp.float32)
    return jnp.clip(values, -6.0, 6.0).astype(jnp.bfloat16)


def draw_w_qkv(key, part):
    key = jax.random.fold_in(key, 2)
    key_base = jax.random.fold_in(key, 0)
    base = jax.random.normal(key_base, (3, D, D), jnp.float32) * D ** (-0.5)
    return jnp.clip(base, -1.0, 1.0).astype(jnp.bfloat16)


def draw_owner_slot(key, part):
    key = jax.random.fold_in(key, 3)
    sources = POOLED // POOLED_DEV
    share_rows = POOLED_DEV // sources
    key_rows, key_slots = jax.random.split(key)
    source_perm = jax.vmap(lambda piece: jax.random.permutation(piece, POOLED_DEV))(jax.random.split(key_rows, sources))
    target_perm = jax.vmap(lambda piece: jax.random.permutation(piece, POOLED_DEV))(jax.random.split(key_slots, sources))
    position = jnp.arange(POOLED_DEV, dtype=jnp.int32)
    owner = position // share_rows
    within = position % share_rows
    source_index = jnp.arange(sources, dtype=jnp.int32)[:, None]
    slot_pick = target_perm[owner[None, :], source_index * share_rows + within[None, :]]
    target = owner[None, :] * POOLED_DEV + slot_pick
    global_rows = source_index * POOLED_DEV + source_perm
    return jnp.zeros((POOLED,), jnp.int32).at[global_rows.reshape(-1)].set(target.reshape(-1).astype(jnp.int32))


def steps_of(rng, dims, cuts, smallest, largest):
    def one(dim, blocks):
        steps = jax.random.uniform(jax.random.fold_in(jax.random.fold_in(rng, 6), dim), (blocks,), jnp.float32, smallest / len(cuts), largest / len(cuts))
        return jnp.repeat(jnp.exp(steps), dims[dim] // blocks).reshape((-1,) + (1,) * (len(dims) - dim - 1))

    gain = one(*cuts[0])
    for cut in cuts[1:]:
        gain = gain * one(*cut)
    return gain


def gaussian(key, extent, scale, most, shards=(), held_as=jnp.bfloat16):
    result = jax.random.normal(key, extent, jnp.float32) * scale
    if len(shards) > 0:
        result = steps_of(key, extent, shards, -0.22, 0.18) * result
    return jnp.clip(result, min=-most, max=most).astype(held_as)


def setup_inputs(seed: int = 0) -> dict:
    arg_keys = jax.random.split(jax.random.key(seed), 8)
    stream = draw_stream(jax.random.fold_in(arg_keys[7], 71), 0)
    norm_gain = jnp.clip(1.0 + 0.18 * jax.random.normal(arg_keys[1], (D,), jnp.float32), 0.1, 1.9)
    w_qkv = draw_w_qkv(jax.random.fold_in(arg_keys[7], 71), 0)
    w_out = gaussian(arg_keys[3], (D, D), D ** -0.5, 0.15625, ((0, 8),))
    pool_gain = jnp.clip(1.0 + 0.18 * jax.random.normal(arg_keys[4], (D,), jnp.float32), 0.1, 1.9)
    w_llm = gaussian(arg_keys[5], (D, LLM_D), D ** -0.5, 0.15625, ((1, 8),))
    owner_slot = draw_owner_slot(jax.random.fold_in(arg_keys[7], 71), 0)
    return dict(stream=stream, norm_gain=norm_gain, w_qkv=w_qkv, w_out=w_out, pool_gain=pool_gain, w_llm=w_llm, owner_slot=owner_slot)


def layer_norm(values, scale_gain):
    average = lax.optimization_barrier(jnp.mean(values, axis=-1, keepdims=True))
    centered = values - average
    spread = lax.optimization_barrier(jnp.mean(centered * centered, axis=-1, keepdims=True))
    return centered * lax.rsqrt(spread + 1e-06) * scale_gain

def reference(stream, norm_gain, w_qkv, w_out, pool_gain, w_llm, owner_slot):
    wide_in = stream.astype(jnp.float32)
    normed = layer_norm(wide_in, norm_gain).astype(jnp.bfloat16)
    projections = jnp.stack([jnp.dot(normed, w_qkv[j], preferred_element_type=jnp.float32) for j in range(3)]).astype(jnp.bfloat16)
    projections = projections.reshape(3, CLIPS, FRAMES, PATCHES, HEADS, HDIM)
    by_head = jnp.moveaxis(projections, 4, 0)
    factor = 1.0 / HDIM ** 0.5

    def one_head(parts):
        query = parts[0].astype(jnp.float32)
        keys = parts[1].astype(jnp.float32)
        values = parts[2].astype(jnp.float32)
        scores = jnp.einsum('cfpe,cgpe->cpfg', query, keys) * factor
        probs = jax.nn.softmax(scores, axis=-1).astype(jnp.bfloat16)
        mixed = jnp.einsum('cpfg,cgpe->cfpe', probs.astype(jnp.float32), values)
        return mixed.astype(jnp.bfloat16)
    attended = lax.map(one_head, by_head)
    attended = jnp.moveaxis(attended, 0, 3).reshape(TOKENS, D)
    pooled_att = attended.reshape(CLIPS * FRAMES // 4, 4, PATCHES, D).astype(jnp.float32).mean(axis=1)
    pooled_att = pooled_att.astype(jnp.bfloat16).reshape(POOLED, D)
    pooled_in = wide_in.reshape(CLIPS * FRAMES // 4, 4, PATCHES, D).mean(axis=1).reshape(POOLED, D)
    merged = pooled_in + jnp.dot(pooled_att, w_out, preferred_element_type=jnp.float32)
    final = layer_norm(merged, pool_gain).astype(jnp.bfloat16)
    projected = jnp.dot(final, w_llm, preferred_element_type=jnp.float32).astype(jnp.bfloat16)
    return jnp.zeros((POOLED, LLM_D), jnp.bfloat16).at[owner_slot].set(projected)
```

```python
import functools
import math

import jax
import jax.numpy as jnp
from jax import lax
from jax.experimental import pallas as pl
from jax.experimental.pallas import tpu as pltpu
from jax.sharding import PartitionSpec as P

MESH = pl.DeviceIdType.MESH
NT = (((1,), (1,)), ((), ()))
HDIM = 88
D = 1408
W = 176
EPS = 1e-6
CHUNKS = 4
BF = jnp.bfloat16
F32 = jnp.float32


def iota(shape, dim):
    return lax.broadcasted_iota(jnp.int32, shape, dim)


def norm_rows(values, gain):
    average = jnp.mean(values, axis=-1, keepdims=True)
    centered = values - average
    spread = jnp.mean(centered * centered, axis=-1, keepdims=True)
    return centered * lax.rsqrt(spread + EPS) * gain


def kernel(
    x_ref, gain_ref, wt_ref, wout_ref, pgain_ref, wllm_ref, rank_ref, place_ref, out_ref,
    xb, nb, qsend, qrecv, tq, tk, tv, att, psend, arecv, wall, xs, fin, proj, fsend, frecv, perm, pool,
    xsem, xssem, qs_sem, qr_sem, ps_sem, pr_sem, ws_sem, wr_sem, wf_sem, wown_sem, fs_sem, fr_sem, os_sem, or_sem,
):
    f = lax.axis_index("frame")
    m = lax.axis_index("mp")
    clip8 = (f // 8) * 8
    j = f % 8
    cx = j // 2
    core = f % 2

    def mate(i):
        step = (1 + i % 3) * (1 - i // 6)
        return ((cx + step) % 4) * 2 + (core + i) % 2

    def source(i):
        step = (1 + i % 3) * (1 - i // 6)
        return ((cx + 4 - step) % 4) * 2 + (core + i) % 2

    def x_copy(i, slot):
        first = mate(i % 8) * 32 + (i // 8) * 16
        return pltpu.make_async_copy(x_ref.at[:, pl.ds(first, 16), :], xb.at[slot], xsem.at[slot])

    for i in range(2):
        x_copy(i, i).start()

    def xs_copy(half):
        return pltpu.make_async_copy(x_ref.at[:, pl.ds(m * 32 + half * 16, 16), :], xs.at[half], xssem.at[half])

    barrier = pltpu.get_barrier_semaphore()

    def greet(i, _):
        pl.semaphore_signal(barrier, inc=1, device_id=((f + i) % 16, m), device_id_type=MESH)
        return 0

    lax.fori_loop(1, 16, greet, 0)

    def greet_mp(i, _):
        pl.semaphore_signal(barrier, inc=1, device_id=(f, (m + i) % 8), device_id_type=MESH)
        return 0

    lax.fori_loop(1, 8, greet_mp, 0)

    def greet_back(i, _):
        @pl.when(jnp.logical_or(j != m, i != m))
        def _():
            pl.semaphore_signal(barrier, inc=1, device_id=(clip8 + m, i), device_id_type=MESH)

        return 0

    lax.fori_loop(0, 8, greet_back, 0)

    row, col = iota((128, 128), 0), iota((128, 128), 1)
    perm[...] = jnp.where((row >> 4 == (col & 7)) & ((row & 15) == col >> 3), 1.0, 0.0).astype(BF)
    row, col = iota((128, 512), 0), iota((128, 512), 1)
    hit = ((col >> 7) == ((row >> 2) & 3)) & (((col & 127) >> 2) == ((row >> 4) * 4 + (row & 3)))
    pool[...] = jnp.where(hit, 0.25, 0.0).astype(BF)
    tv[...] = jnp.where(iota((8, 128, 256), 2) == W, 1.0, 0.0).astype(BF)

    @pl.when(j == m)
    def _():
        pl.semaphore_wait(barrier, 29)

    @pl.when(j != m)
    def _():
        pl.semaphore_wait(barrier, 30)

    def w_copy(e):
        return pltpu.make_async_remote_copy(
            src_ref=wout_ref, dst_ref=wall.at[m], send_sem=ws_sem.at[e], recv_sem=wr_sem.at[e],
            device_id=(f, (m + e) % 8), device_id_type=MESH,
        )

    def w_pass(e):
        shard = wall.at[(m + 8 - e) % 8]
        return pltpu.make_async_remote_copy(
            src_ref=shard, dst_ref=shard, send_sem=ws_sem.at[e], recv_sem=wf_sem.at[e],
            device_id=(f + 1 - 2 * core, m), device_id_type=MESH,
        )

    def q_copy(i, half):
        to = mate(i % 8)
        chunk = (i // 8) * 2 + half
        return pltpu.make_async_remote_copy(
            src_ref=qsend.at[i, half], dst_ref=qrecv.at[chunk, j], send_sem=qs_sem.at[i, half],
            recv_sem=qr_sem.at[chunk, i % 8], device_id=(clip8 + to, m), device_id_type=MESH,
        )

    def q_own(i, half):
        chunk = (i // 8) * 2 + half
        return pltpu.make_async_copy(qsend.at[i, half], qrecv.at[chunk, j], qr_sem.at[chunk, 6])

    def q_start(i, half):
        @pl.when(i % 8 == 6)
        def _():
            q_own(i, half).start()

        @pl.when(i % 8 != 6)
        def _():
            q_copy(i, half).start()

    def project(i, _):
        slot = i % 2
        x_copy(i, slot).wait()

        def frames(t, _):
            y = norm_rows(xb[slot, pl.ds(2 * t, 2)].astype(F32).reshape(32, D), gain_ref[...])
            y = y.reshape(2, 2, 8, D)
            rows = pl.ds(pl.multiple_of(16 * t, 16), 16)
            nb[0, rows, :] = y[:, 0].reshape(16, D).astype(BF)
            nb[1, rows, :] = y[:, 1].reshape(16, D).astype(BF)
            return 0

        lax.fori_loop(0, 8, frames, 0, unroll=2)

        @pl.when(i + 2 < 16)
        def _():
            x_copy(i + 2, slot).start()

        qkv = lax.dot_general(wt_ref[...], nb[...].reshape(256, D), NT, preferred_element_type=F32)
        qsend[i, 0] = qkv[:, :128].astype(BF)
        qsend[i, 1] = qkv[:, 128:].astype(BF)
        q_start(i, 0)

        @pl.when(i < 8)
        def _():
            q_start(i, 1)

        return 0

    lax.fori_loop(0, 4, project, 0)
    own_w = pltpu.make_async_copy(wout_ref, wall.at[m], wown_sem)
    own_w.start()
    for half in range(2):
        xs_copy(half).start()
    for e in range(1, 8):

        @pl.when(core == e % 2)
        def _(e=e):
            w_copy(e).start()

    lax.fori_loop(4, 16, project, 0)

    def late(i, _):
        q_start(i, 1)
        return 0

    lax.fori_loop(8, 16, late, 0)

    def p_copy(chunk, i):
        to = (j + i) % 8
        rows = pl.ds(pl.multiple_of(chunk * 32, 32), 32)
        return pltpu.make_async_remote_copy(
            src_ref=psend.at[to, rows], dst_ref=arecv.at[m, rows], send_sem=ps_sem.at[chunk, i],
            recv_sem=pr_sem.at[chunk, m], device_id=(clip8 + to, j), device_id_type=MESH,
        )

    def p_own(chunk):
        rows = pl.ds(pl.multiple_of(chunk * 32, 32), 32)
        return pltpu.make_async_copy(psend.at[j, rows], arecv.at[m, rows], pr_sem.at[chunk, m])

    def attend(chunk):
        def turn(i, _):
            pltpu.make_async_copy(qsend.at[0, 0], qrecv.at[chunk, source(i)], qr_sem.at[chunk, i]).wait()
            s = source(i)
            block = qrecv.at[chunk, s]
            rows = pl.ds(pl.multiple_of(s * 16, 16), 16)
            for k, to in enumerate((tq, tk, tv)):
                part = lax.dot_general(perm[...], block[k * W : (k + 1) * W, :], NT, preferred_element_type=F32)
                to[:, rows, 0:W] = part.astype(BF).reshape(8, 16, W)
            return 0

        lax.fori_loop(0, 8, turn, 0)

        def quad(n, _):
            first = iota((128, W), 1) < HDIM
            wide = iota((128, 256), 1) < HDIM
            scale = math.log2(math.e) / math.sqrt(HDIM)
            for p in range(4):
                q = tq[4 * n + p]
                zero = jnp.zeros_like(q)
                q2 = jnp.concatenate([jnp.where(first, q, zero), jnp.where(first, zero, q)], axis=0)
                s = lax.dot_general(q2, tk[4 * n + p], NT, preferred_element_type=F32)
                top = jnp.max(s, axis=-1, keepdims=True)
                e = jnp.exp2((s - top) * scale).astype(BF)
                o = jnp.dot(e, tv[4 * n + p], preferred_element_type=F32)
                o = o * (1.0 / o[:, W : W + 1])
                att[p * 128 : (p + 1) * 128, :] = jnp.where(wide, o[:128], o[128:]).astype(BF)
            mean = jnp.dot(pool[...], att[...], preferred_element_type=F32).astype(BF)
            psend[:, pl.ds(pl.multiple_of(chunk * 32 + n * 16, 16), 16), :] = mean.reshape(8, 16, 256)
            return 0

        lax.fori_loop(0, 2, quad, 0)

        def back(i, _):
            here = jnp.logical_and(i == 0, j == m)

            @pl.when(here)
            def _():
                p_own(chunk).start()

            @pl.when(jnp.logical_not(here))
            def _():
                p_copy(chunk, i).start()

            return 0

        lax.fori_loop(0, 8, back, 0)

    def f_copy(chunk, e):
        rows = fin.at[m, pl.ds(pl.multiple_of(chunk * 32, 32), 32)]
        return pltpu.make_async_remote_copy(
            src_ref=rows, dst_ref=rows, send_sem=fs_sem.at[chunk, e], recv_sem=fr_sem.at[chunk, e],
            device_id=(f, (m + e) % 8), device_id_type=MESH,
        )

    def merge(chunk):
        rows = pl.ds(pl.multiple_of(chunk * 32, 32), 32)
        row, col = iota((32, 256), 0), iota((32, 256), 1)
        hit = ((col & 15) == (chunk % 2) * 8 + (row >> 2)) & ((col >> 6) == (row & 3))
        total = jnp.dot(
            jnp.where(hit, 0.25, 0.0).astype(BF), xs[chunk // 2].reshape(256, D), preferred_element_type=F32
        )
        for s in range(8):
            pltpu.make_async_copy(psend.at[0, rows], arecv.at[s, rows], pr_sem.at[chunk, s]).wait()
        for s in range(8):
            total += jnp.dot(arecv[s, rows, 0:W], wall[s], preferred_element_type=F32)
        fin[m, rows, :] = norm_rows(total, pgain_ref[...]).astype(BF)

        def spread(e, _):
            f_copy(chunk, e).start()
            return 0

        lax.fori_loop(1, 8, spread, 0)

    attend(0)
    for e in range(1, 8):

        @pl.when(core == e % 2)
        def _(e=e):
            w_copy(e).wait()
            w_pass(e).start()

    def middle(chunk, _):
        attend(chunk)

        @pl.when(chunk == 1)
        def _():
            own_w.wait()
            for half in range(2):
                xs_copy(half).wait()
            for e in range(1, 8):

                @pl.when(core == e % 2)
                def _(e=e):
                    w_pass(e).wait_send()

                @pl.when(core != e % 2)
                def _(e=e):
                    w_pass(e).wait_recv()

        merge(chunk - 1)
        return 0

    lax.fori_loop(1, CHUNKS, middle, 0)

    order = jnp.where(iota((1024, 1024), 0) == rank_ref[...], 1.0, 0.0).astype(BF)
    merge(CHUNKS - 1)

    def arrived(n, _):
        f_copy(n // 8, 1 + n % 8).wait_recv()
        return 0

    for chunk in range(CHUNKS):
        for e in range(1, 8):
            f_copy(chunk, e).wait_recv()

    def o_copy(half, i):
        to = (f + i) % 16
        return pltpu.make_async_remote_copy(
            src_ref=fsend.at[half, to], dst_ref=frecv.at[half, f], send_sem=os_sem.at[half, i],
            recv_sem=or_sem.at[half, i], device_id=(to, m), device_id_type=MESH,
        )

    for half in range(2):
        lanes = slice(half * 256, half * 256 + 256)
        for s in range(8):
            proj[s * 128 : (s + 1) * 128, :] = jnp.dot(
                fin[s], wllm_ref[:, lanes], preferred_element_type=F32
            ).astype(BF)
        turned = jnp.dot(order, proj[...], preferred_element_type=F32).astype(BF)
        fsend[half] = turned.reshape(16, 64, 256)

        def share(i, _, half=half):
            o_copy(half, i).start()
            return 0

        lax.fori_loop(1, 16, share, 0)
        frecv[half, f] = fsend[half, f]

    place = jnp.where(iota((1024, 1024), 0) == place_ref[...], 1.0, 0.0).astype(BF)
    for half in range(2):

        def landed(i, _, half=half):
            o_copy(half, i).wait_recv()
            return 0

        lax.fori_loop(1, 16, landed, 0)
        out_ref[:, half * 256 : half * 256 + 256] = jnp.dot(
            place, frecv[half].reshape(1024, 256), preferred_element_type=F32
        ).astype(BF)

    def left_q(i, _):
        @pl.when(i % 8 != 6)
        def _():
            q_copy(i, 0).wait_send()
            q_copy(i, 1).wait_send()

        return 0

    lax.fori_loop(0, 16, left_q, 0)

    def left_p(i, _):
        @pl.when(jnp.logical_not(jnp.logical_and(i == 0, j == m)))
        def _():
            for chunk in range(CHUNKS):
                p_copy(chunk, i).wait_send()

        return 0

    lax.fori_loop(0, 8, left_p, 0)

    def left_f(e, _):
        for chunk in range(CHUNKS):
            f_copy(chunk, e).wait_send()
        return 0

    lax.fori_loop(1, 8, left_f, 0)

    def left_o(i, _):
        for half in range(2):
            o_copy(half, i).wait_send()
        return 0

    lax.fori_loop(1, 16, left_o, 0)


def per_device(stream, norm_gain, w_qkv, w_out, pool_gain, w_llm, owner_slot):
    own = lax.axis_index("frame")
    frames = stream.reshape(16, 256, D)
    wt = jnp.swapaxes(w_qkv, 1, 2).reshape(3 * W, D)
    blocks = owner_slot.reshape(16, 1024)
    mine = lax.dynamic_index_in_dim(blocks, own, 0, keepdims=False)
    mine = mine.reshape(4, 256).T.reshape(1024)
    rank = jnp.sum((mine[:, None] < mine[None, :]).astype(jnp.int32), axis=0)[None]
    ordered = jnp.sort(blocks, axis=1)
    place = lax.dynamic_slice_in_dim(ordered, own * 64, 64, 1).reshape(1, 1024) - own * 1024
    vmem = pl.BlockSpec(memory_space=pltpu.VMEM)
    dma = pltpu.SemaphoreType.DMA
    return pl.pallas_call(
        kernel,
        out_shape=jax.ShapeDtypeStruct((1024, 512), BF),
        in_specs=[pl.BlockSpec(memory_space=pl.ANY)] + [vmem] * 7,
        out_specs=vmem,
        scratch_shapes=[
            pltpu.VMEM((2, 16, 16, D), BF),
            pltpu.VMEM((2, 128, D), BF),
            pltpu.VMEM((16, 2, 3 * W, 128), BF),
            pltpu.VMEM((4, 8, 3 * W, 128), BF),
            pltpu.VMEM((8, 128, W), BF),
            pltpu.VMEM((8, 128, W), BF),
            pltpu.VMEM((8, 128, 256), BF),
            pltpu.VMEM((512, 256), BF),
            pltpu.VMEM((8, 128, 256), BF),
            pltpu.VMEM((8, 128, 256), BF),
            pltpu.VMEM((8, W, D), BF),
            pltpu.VMEM((2, 16, 16, D), BF),
            pltpu.VMEM((8, 128, D), BF),
            pltpu.VMEM((1024, 256), BF),
            pltpu.VMEM((2, 16, 64, 256), BF),
            pltpu.VMEM((2, 16, 64, 256), BF),
            pltpu.VMEM((128, 128), BF),
            pltpu.VMEM((128, 512), BF),
            dma((2,)), dma((2,)), dma((16, 2)), dma((4, 8)), dma((4, 8)), dma((4, 8)),
            dma((8,)), dma((8,)), dma((8,)), dma, dma((4, 8)), dma((4, 8)), dma((2, 16)), dma((2, 16)),
        ],
        compiler_params=pltpu.CompilerParams(
            collective_id=0, has_side_effects=True, vmem_limit_bytes=56 * 2**20
        ),
        name="video_layer",
    )(frames, norm_gain[None], wt, w_out, pool_gain[None], w_llm, rank, place)


def solution(mesh):
    return jax.shard_map(
        per_device,
        mesh=mesh,
        in_specs=(
            P("frame", None), P(), P(None, None, "mp"), P("mp", None), P(), P(None, "mp"), P(),
        ),
        out_specs=P("frame", "mp"),
        check_vma=False,
    )
```

```python
import functools
import math

import jax
import jax.numpy as jnp
from jax import lax
from jax.experimental import pallas as pl
from jax.experimental.pallas import tpu as pltpu
from jax.sharding import PartitionSpec as P

MESH = pl.DeviceIdType.MESH
NT = (((1,), (1,)), ((), ()))
HDIM = 88
D = 1408
W = 176
EPS = 1e-6
CHUNKS = 4
FAR = sorted(((a, b, c) for a in (0, 1) for b in range(4) for c in (0, 1) if (a, b, c) != (0, 0, 0)), key=lambda s: -s[0] - min(s[1], 4 - s[1]))
BF = jnp.bfloat16
F32 = jnp.float32


def iota(shape, dim):
    return lax.broadcasted_iota(jnp.int32, shape, dim)


def norm_rows(values, gain):
    average = jnp.mean(values, axis=-1, keepdims=True)
    centered = values - average
    spread = jnp.mean(centered * centered, axis=-1, keepdims=True)
    return centered * lax.rsqrt(spread + EPS) * gain


def kernel(
    x_ref, gain_ref, wt_hbm, wout_hbm, pgain_ref, wllm_hbm, slot_ref, out_ref,
    wt_ref, wout_ref, wllm_ref, xb, nb0, nb1, qsend, qrecv, tq, tk, tv, att, psend, arecv, wall, xs, fin, proj, total, order, place, fsend, frecv, perm, pool,
    in_sem, xsem, xssem, qs_sem, qr_sem, ps_sem, pr_sem, ws_sem, wr_sem, wp_sem, wf_sem, wown_sem, fs_sem, fr_sem, os_sem, or_sem,
):
    f = lax.axis_index("frame")
    m = lax.axis_index("mp")
    clip8 = (f // 8) * 8
    j = f % 8
    cx = j // 2
    core = f % 2

    def mate(i):
        step = (1 + i % 3) * (1 - i // 6)
        return ((cx + step) % 4) * 2 + (core + i) % 2

    def source(i):
        step = (1 + i % 3) * (1 - i // 6)
        return ((cx + 4 - step) % 4) * 2 + (core + i) % 2

    def x_copy(i, slot):
        first = mate(i % 8) * 32 + (i // 8) * 16
        return pltpu.make_async_copy(x_ref.at[:, pl.ds(first, 16), :], xb.at[slot], xsem.at[slot])

    def w_in(n):
        ends = ((wt_hbm, wt_ref), (wout_hbm, wout_ref), (wllm_hbm, wllm_ref))[n]
        return pltpu.make_async_copy(*ends, in_sem.at[n])

    x_copy(0, 0).start()
    w_in(0).start()
    x_copy(1, 1).start()
    w_in(1).start()
    w_in(2).start()

    def xs_copy(half):
        return pltpu.make_async_copy(x_ref.at[:, pl.ds(m * 32 + half * 16, 16), :], xs.at[half], xssem.at[half])

    barrier = pltpu.get_barrier_semaphore()

    def greet(i, _):
        pl.semaphore_signal(barrier, inc=1, device_id=((f + i) % 16, m), device_id_type=MESH)
        return 0

    lax.fori_loop(1, 16, greet, 0)

    def greet_mp(i, _):
        pl.semaphore_signal(barrier, inc=1, device_id=(f, (m + i) % 8), device_id_type=MESH)
        return 0

    lax.fori_loop(1, 8, greet_mp, 0)

    def greet_back(i, _):
        @pl.when(jnp.logical_or(j != m, i != m))
        def _():
            pl.semaphore_signal(barrier, inc=1, device_id=(clip8 + m, i), device_id_type=MESH)

        return 0

    lax.fori_loop(0, 8, greet_back, 0)

    row, col = iota((128, 128), 0), iota((128, 128), 1)
    perm[...] = jnp.where((row >> 4 == (col & 7)) & ((row & 15) == col >> 3), 1.0, 0.0).astype(BF)
    row, col = iota((128, 512), 0), iota((128, 512), 1)
    hit = ((col >> 7) == ((row >> 2) & 3)) & (((col & 127) >> 2) == ((row >> 4) * 4 + (row & 3)))
    pool[...] = jnp.where(hit, 0.25, 0.0).astype(BF)
    tv[...] = jnp.where(iota((8, 128, 256), 2) == W, 1.0, 0.0).astype(BF)

    zh, y = m // 4, m % 4
    across = (m + 4) % 8

    def ring(k):
        return zh * 4 + (y + k) % 4

    def behind(k):
        return zh * 4 + (y + 4 - k) % 4

    def w_z():
        return pltpu.make_async_remote_copy(
            src_ref=wout_ref, dst_ref=wall.at[m], send_sem=ws_sem.at[0], recv_sem=wr_sem.at[0],
            device_id=(f, across), device_id_type=MESH,
        )

    def w_y(k):
        return pltpu.make_async_remote_copy(
            src_ref=wout_ref, dst_ref=wall.at[m], send_sem=ws_sem.at[k], recv_sem=wr_sem.at[k],
            device_id=(f, ring(k)), device_id_type=MESH,
        )

    def w_on(k):
        return pltpu.make_async_remote_copy(
            src_ref=wall.at[across], dst_ref=wall.at[across], send_sem=ws_sem.at[k], recv_sem=wr_sem.at[k],
            device_id=(f, ring(k)), device_id_type=MESH,
        )

    def w_pass(k, shard):
        return pltpu.make_async_remote_copy(
            src_ref=wall.at[shard], dst_ref=wall.at[shard], send_sem=wp_sem.at[k], recv_sem=wf_sem.at[k],
            device_id=(f + 1 - 2 * core, m), device_id_type=MESH,
        )

    def q_copy(i, half):
        to = mate(i % 8)
        chunk = (i // 8) * 2 + half
        return pltpu.make_async_remote_copy(
            src_ref=qsend.at[i, half], dst_ref=qrecv.at[chunk, j], send_sem=qs_sem.at[i, half],
            recv_sem=qr_sem.at[chunk, i % 8], device_id=(clip8 + to, m), device_id_type=MESH,
        )

    def q_own(i, half):
        chunk = (i // 8) * 2 + half
        return pltpu.make_async_copy(qsend.at[i, half], qrecv.at[chunk, j], qr_sem.at[chunk, 6])

    def q_start(i, half):
        @pl.when(i % 8 == 6)
        def _():
            q_own(i, half).start()

        @pl.when(i % 8 != 6)
        def _():
            q_copy(i, half).start()

    def normalize(slot, to):
        for n in range(8):
            v = norm_rows(xb[slot, 2 * n : 2 * n + 2].astype(F32).reshape(32, D), gain_ref[...].reshape(1, D))
            v = v.reshape(2, 2, 8, D)
            to[16 * n : 16 * n + 16, :] = v[:, 0].reshape(16, D).astype(BF)
            to[128 + 16 * n : 144 + 16 * n, :] = v[:, 1].reshape(16, D).astype(BF)

    def project(i, now, later, slot):
        @pl.when(i + 1 < 16)
        def _():
            x_copy(i + 1, slot).wait()

        qkv = lax.dot_general(wt_ref[...], now[...], NT, preferred_element_type=F32)
        qsend[i, 0] = qkv[:, :128].astype(BF)
        qsend[i, 1] = qkv[:, 128:].astype(BF)
        normalize(slot, later)

        @pl.when(i + 3 < 16)
        def _():
            x_copy(i + 3, slot).start()

    def two(n, _):
        project(2 * n, nb0, nb1, 1)
        project(2 * n + 1, nb1, nb0, 0)
        return 0

    def two_sent(n, _):
        two(n, 0)
        q_start(2 * n, 0)
        q_start(2 * n + 1, 0)
        return 0

    w_in(0).wait()
    x_copy(0, 0).wait()
    normalize(0, nb0)
    x_copy(2, 0).start()
    lax.fori_loop(0, 2, two, 0)
    w_in(1).wait()
    w_in(2).wait()

    @pl.when(j == m)
    def _():
        pl.semaphore_wait(barrier, 29)

    @pl.when(j != m)
    def _():
        pl.semaphore_wait(barrier, 30)

    def first(i, _):
        q_start(i, 0)
        return 0

    lax.fori_loop(0, 4, first, 0)

    @pl.when(core == 0)
    def _():
        for k in range(1, 4):
            w_y(k).start()

    @pl.when(core == 1)
    def _():
        w_z().start()

    def two_later(n, _):
        two(n, 0)
        q_start(2 * n - 8, 1)
        q_start(2 * n - 7, 1)
        return 0

    lax.fori_loop(2, 4, two_sent, 0)
    lax.fori_loop(4, 6, two_later, 0)

    @pl.when(core == 1)
    def _():
        w_z().wait()
        for k in range(1, 4):
            w_on(k).start()

    own_w = pltpu.make_async_copy(wout_ref, wall.at[m], wown_sem)
    own_w.start()
    for half in range(2):
        xs_copy(half).start()
    lax.fori_loop(6, 8, two_later, 0)

    def p_copy(chunk, i):
        to = (j + i) % 8
        rows = pl.ds(pl.multiple_of(chunk * 32, 32), 32)
        return pltpu.make_async_remote_copy(
            src_ref=psend.at[to, rows], dst_ref=arecv.at[m, rows], send_sem=ps_sem.at[chunk, i],
            recv_sem=pr_sem.at[chunk, m], device_id=(clip8 + to, j), device_id_type=MESH,
        )

    def p_own(chunk):
        rows = pl.ds(pl.multiple_of(chunk * 32, 32), 32)
        return pltpu.make_async_copy(psend.at[j, rows], arecv.at[m, rows], pr_sem.at[chunk, m])

    def attend(chunk, feed=None):
        def turn(i, _):
            pltpu.make_async_copy(qsend.at[0, 0], qrecv.at[chunk, source(i)], qr_sem.at[chunk, i]).wait()
            if feed is not None:
                q_start(8 + i, feed)
            s = source(i)
            block = qrecv.at[chunk, s]
            rows = pl.ds(pl.multiple_of(s * 16, 16), 16)
            for k, to in enumerate((tq, tk, tv)):
                part = lax.dot_general(perm[...], block[k * W : (k + 1) * W, :], NT, preferred_element_type=F32)
                to[:, rows, 0:W] = part.astype(BF).reshape(8, 16, W)
            return 0

        lax.fori_loop(0, 8, turn, 0)

        def quad(n, _):
            first = iota((128, W), 1) < HDIM
            wide = iota((128, 256), 1) < HDIM
            scale = math.log2(math.e) / math.sqrt(HDIM)
            for p in range(4):
                q = tq[4 * n + p]
                zero = jnp.zeros_like(q)
                q2 = jnp.concatenate([jnp.where(first, q, zero), jnp.where(first, zero, q)], axis=0)
                s = lax.dot_general(q2, tk[4 * n + p], NT, preferred_element_type=F32)
                top = jnp.max(s, axis=-1, keepdims=True)
                e = jnp.exp2((s - top) * scale).astype(BF)
                o = jnp.dot(e, tv[4 * n + p], preferred_element_type=F32)
                o = o * (1.0 / o[:, W : W + 1])
                att[p * 128 : (p + 1) * 128, :] = jnp.where(wide, o[:128], o[128:]).astype(BF)
            mean = jnp.dot(pool[...], att[...], preferred_element_type=F32).astype(BF)
            psend[:, pl.ds(pl.multiple_of(chunk * 32 + n * 16, 16), 16), :] = mean.reshape(8, 16, 256)
            return 0

        lax.fori_loop(0, 2, quad, 0)

        def back(i, _):
            here = jnp.logical_and(i == 0, j == m)

            @pl.when(here)
            def _():
                p_own(chunk).start()

            @pl.when(jnp.logical_not(here))
            def _():
                p_copy(chunk, i).start()

            return 0

        lax.fori_loop(0, 8, back, 0)

    def f_copy(chunk, e):
        owner = across if e > 3 else m
        rows = fin.at[owner, pl.ds(pl.multiple_of(chunk * 32, 32), 32)]
        return pltpu.make_async_remote_copy(
            src_ref=rows, dst_ref=rows, send_sem=fs_sem.at[chunk, e], recv_sem=fr_sem.at[chunk, e],
            device_id=(f, across if e == 0 else ring((e - 1) % 3 + 1)), device_id_type=MESH,
        )

    def pass_on(chunk):
        f_copy(chunk, 0).wait_recv()
        for e in range(4, 7):
            f_copy(chunk, e).start()

    def merge(chunk):
        rows = pl.ds(pl.multiple_of(chunk * 32, 32), 32)
        row, col = iota((32, 256), 0), iota((32, 256), 1)
        hit = ((col & 15) == (chunk % 2) * 8 + (row >> 2)) & ((col >> 6) == (row & 3))
        merged = jnp.dot(
            jnp.where(hit, 0.25, 0.0).astype(BF), xs[chunk // 2].reshape(256, D), preferred_element_type=F32
        )
        for s in range(8):
            pltpu.make_async_copy(psend.at[0, rows], arecv.at[s, rows], pr_sem.at[chunk, s]).wait()
        for s in range(8):
            merged += jnp.dot(arecv[s, rows, 0:W], wall[s], preferred_element_type=F32)
        fin[m, rows, :] = norm_rows(merged, pgain_ref[...].reshape(1, D)).astype(BF)

        for e in range(4):
            f_copy(chunk, e).start()

    def sort_rows():
        mine = slot_ref[pl.ds(pl.multiple_of(f * 8, 8), 8), :]
        parts = jnp.concatenate([mine >> 7, mine & 127], axis=0).astype(F32).astype(BF)
        lane, spot = iota((128, 1024), 0), iota((128, 1024), 1)
        patch = ((spot >> 5) & 3) * 32 + (spot >> 8) * 8 + ((spot >> 2) & 7)
        pick = jnp.where(patch == lane, 1.0, 0.0).astype(BF)
        picked = jnp.dot(parts, pick, preferred_element_type=F32)
        picked = picked[:8] * 128.0 + picked[8:]
        group, spot = iota((8, 1024), 0), iota((8, 1024), 1)
        keep = group == (spot & 3) * 2 + ((spot >> 7) & 1)
        along = jnp.sum(jnp.where(keep, picked, 0.0), axis=0, keepdims=True)
        same = jnp.where(iota((128, 128), 0) == iota((128, 128), 1), 1.0, 0.0).astype(BF)
        down = lax.dot_general(same, parts, NT, preferred_element_type=F32)
        down = down[:, :8] * 128.0 + down[:, 8:]
        count = jnp.zeros((128, 1024), F32)
        for n in range(8):
            count += jnp.where(down[:, n : n + 1] < along, 1.0, 0.0)
        rank = jnp.sum(count, axis=0, keepdims=True).astype(jnp.int32)

        def fill(n, _):
            rows = pl.ds(pl.multiple_of(n * 128, 128), 128)
            order[rows, :] = jnp.where(iota((128, 1024), 0) + n * 128 == rank, 1.0, 0.0).astype(BF)
            return 0

        lax.fori_loop(0, 8, fill, 0)

    def place_rows():
        def block(b, found):
            slots = slot_ref[pl.ds(pl.multiple_of(b * 8, 8), 8), :]
            high = (slots >> 7) - f * 8
            high = jnp.where((high >= 0) & (high < 8), high + b * 8, -1)
            low = slots & 127
            row = iota((128, 128), 0)
            highs = [jnp.where(high[n : n + 1] == row, 1.0, 0.0).astype(BF) for n in range(8)]
            lows = [jnp.where(low[n : n + 1] == row, 1.0, 0.0).astype(BF) for n in range(8)]
            return found + lax.dot_general(
                jnp.concatenate(lows, axis=1), jnp.concatenate(highs, axis=1), NT, preferred_element_type=F32
            )

        found = lax.fori_loop(0, 16, block, jnp.zeros((128, 128), F32))
        row, col = iota((128, 128), 0), iota((128, 128), 1)
        marks = found.astype(BF)
        before = jnp.where(row > col, 1.0, 0.0).astype(BF)
        rank = jnp.dot(before, marks, preferred_element_type=F32)
        sums = jnp.dot(jnp.ones((128, 128), BF), marks, preferred_element_type=F32).astype(BF)
        lower = jnp.where((row >> 3 == col >> 3) & (row < col), 1.0, 0.0).astype(BF)
        rank += jnp.dot(sums, lower, preferred_element_type=F32)
        key = found * (rank + ((col >> 3) * 64).astype(F32))
        for n in range(8):
            at = jnp.sum(jnp.where((col & 7) == n, key, 0.0), axis=1, keepdims=True).astype(jnp.int32)
            place[n * 128 : n * 128 + 128, :] = jnp.where(iota((128, 1024), 1) == at, 1.0, 0.0).astype(BF)

    sort_rows()
    place_rows()
    attend(0)

    own_w.wait()
    for half in range(2):
        xs_copy(half).wait()

    @pl.when(core == 0)
    def _():
        for k in range(1, 4):
            w_y(k).wait()
            w_pass(k, behind(k)).start()

    @pl.when(core == 1)
    def _():
        w_pass(0, across).start()
        for k in range(1, 4):
            w_on(k).wait()
            w_pass(k, (behind(k) + 4) % 8).start()

    attend(1, 0)

    @pl.when(core == 0)
    def _():
        for k in range(1, 4):
            w_pass(k, behind(k)).wait_send()
        w_pass(0, across).wait_recv()
        for k in range(1, 4):
            w_pass(k, (behind(k) + 4) % 8).wait_recv()

    @pl.when(core == 1)
    def _():
        w_pass(0, across).wait_send()
        for k in range(1, 4):
            w_pass(k, (behind(k) + 4) % 8).wait_send()
        for k in range(1, 4):
            w_pass(k, behind(k)).wait_recv()

    def read_out(chunk):
        f_rows = pl.ds(pl.multiple_of(chunk * 32, 32), 32)
        for e in range(1, 7):
            f_copy(chunk, e).wait_recv()
        rows = pl.ds(pl.multiple_of(chunk * 256, 256), 256)
        proj[rows, :] = jnp.dot(
            fin[:, f_rows, :].reshape(256, D), wllm_ref[...], preferred_element_type=F32
        ).astype(BF)

    merge(0)
    attend(2, 1)
    pass_on(0)
    merge(1)
    attend(3)
    merge(2)
    pass_on(1)
    merge(3)
    pass_on(2)
    read_out(0)
    pass_on(3)
    read_out(1)

    read_out(2)
    total[...] = jnp.dot(order[:, :768], proj[:768, :], preferred_element_type=F32)
    read_out(3)

    def o_copy(half, i):
        a, b, c = FAR[i]
        to = ((f // 8 + a) % 2) * 8 + ((cx + b) % 4) * 2 + (core + c) % 2
        return pltpu.make_async_remote_copy(
            src_ref=fsend.at[half, to], dst_ref=frecv.at[half, f], send_sem=os_sem.at[half, i],
            recv_sem=or_sem.at[half, i], device_id=(to, m), device_id_type=MESH,
        )

    for half in range(2):
        lanes = slice(half * 256, half * 256 + 256)
        turned = total[:, lanes] + jnp.dot(order[:, 768:], proj[768:, lanes], preferred_element_type=F32)
        fsend[half] = turned.astype(BF).reshape(16, 64, 256)
        for i in range(15):
            o_copy(half, i).start()
        frecv[half, f] = fsend[half, f]

    for half in range(2):
        for i in range(15):
            o_copy(half, i).wait_recv()
        out_ref[:, half * 256 : half * 256 + 256] = jnp.dot(
            place[...], frecv[half].reshape(1024, 256), preferred_element_type=F32
        ).astype(BF)

    def left_q(i, _):
        @pl.when(i % 8 != 6)
        def _():
            q_copy(i, 0).wait_send()
            q_copy(i, 1).wait_send()

        return 0

    lax.fori_loop(0, 16, left_q, 0)

    def left_p(i, _):
        @pl.when(jnp.logical_not(jnp.logical_and(i == 0, j == m)))
        def _():
            for chunk in range(CHUNKS):
                p_copy(chunk, i).wait_send()

        return 0

    lax.fori_loop(0, 8, left_p, 0)

    for chunk in range(CHUNKS):
        for e in range(7):
            f_copy(chunk, e).wait_send()
    for half in range(2):
        for i in range(15):
            o_copy(half, i).wait_send()


def per_device(stream, norm_gain, w_qkv, w_out, pool_gain, w_llm, owner_slot):
    frames = stream.reshape(16, 256, D)
    wt = jnp.swapaxes(w_qkv, 1, 2).reshape(3 * W, D)
    vmem, hbm = pl.BlockSpec(memory_space=pltpu.VMEM), pl.BlockSpec(memory_space=pl.ANY)
    dma = pltpu.SemaphoreType.DMA
    return pl.pallas_call(
        kernel,
        out_shape=jax.ShapeDtypeStruct((1024, 512), BF),
        in_specs=[hbm, vmem, hbm, hbm, vmem, hbm, vmem],
        out_specs=vmem,
        scratch_shapes=[
            pltpu.VMEM((3 * W, D), BF),
            pltpu.VMEM((W, D), BF),
            pltpu.VMEM((D, 512), BF),
            pltpu.VMEM((2, 16, 16, D), BF),
            pltpu.VMEM((256, D), BF),
            pltpu.VMEM((256, D), BF),
            pltpu.VMEM((16, 2, 3 * W, 128), BF),
            pltpu.VMEM((4, 8, 3 * W, 128), BF),
            pltpu.VMEM((8, 128, W), BF),
            pltpu.VMEM((8, 128, W), BF),
            pltpu.VMEM((8, 128, 256), BF),
            pltpu.VMEM((512, 256), BF),
            pltpu.VMEM((8, 128, 256), BF),
            pltpu.VMEM((8, 128, 256), BF),
            pltpu.VMEM((8, W, D), BF),
            pltpu.VMEM((2, 16, 16, D), BF),
            pltpu.VMEM((8, 128, D), BF),
            pltpu.VMEM((1024, 512), BF),
            pltpu.VMEM((1024, 512), F32),
            pltpu.VMEM((1024, 1024), BF),
            pltpu.VMEM((1024, 1024), BF),
            pltpu.VMEM((2, 16, 64, 256), BF),
            pltpu.VMEM((2, 16, 64, 256), BF),
            pltpu.VMEM((128, 128), BF),
            pltpu.VMEM((128, 512), BF),
            dma((3,)), dma((2,)), dma((2,)), dma((16, 2)), dma((4, 8)), dma((4, 8)), dma((4, 8)),
            dma((4,)), dma((4,)), dma((4,)), dma((4,)), dma, dma((4, 8)), dma((4, 8)), dma((2, 16)), dma((2, 16)),
        ],
        compiler_params=pltpu.CompilerParams(
            collective_id=0, has_side_effects=True, vmem_limit_bytes=56 * 2**20
        ),
        name="video_layer",
    )(frames, norm_gain, wt, w_out, pool_gain, w_llm, owner_slot.reshape(128, 128))


def solution(mesh):
    return jax.shard_map(
        per_device,
        mesh=mesh,
        in_specs=(
            P("frame", None), P(), P(None, None, "mp"), P("mp", None), P(), P(None, "mp"), P(),
        ),
        out_specs=P("frame", "mp"),
        check_vma=False,
    )
```

```python
import functools
import math

import jax
import jax.numpy as jnp
from jax import lax
from jax.experimental import pallas as pl
from jax.experimental.pallas import tpu as pltpu
from jax.sharding import PartitionSpec as P

MESH = pl.DeviceIdType.MESH
NT = (((1,), (1,)), ((), ()))
HDIM = 88
D = 1408
W = 176
EPS = 1e-6
CHUNKS = 4
FAR = sorted(((a, b, c) for a in (0, 1) for b in range(4) for c in (0, 1) if (a, b, c) != (0, 0, 0)), key=lambda s: -s[0] - min(s[1], 4 - s[1]))
BF = jnp.bfloat16
F32 = jnp.float32


def iota(shape, dim):
    return lax.broadcasted_iota(jnp.int32, shape, dim)


def norm_rows(values, gain):
    average = jnp.mean(values, axis=-1, keepdims=True)
    centered = values - average
    spread = jnp.mean(centered * centered, axis=-1, keepdims=True)
    return centered * lax.rsqrt(spread + EPS) * gain


def kernel(
    x_ref, gain_ref, wt_hbm, wout_hbm, pgain_ref, wllm_hbm, slot_ref, out_ref,
    wt_ref, wout_ref, wllm_ref, xb, nb0, nb1, qsend, qrecv, tq, tk, tv, att, psend, arecv, wall, xs, fin, proj, total, order, place, fsend, frecv, perm, pool,
    in_sem, xsem, xssem, qs_sem, qr_sem, ps_sem, pr_sem, ws_sem, wr_sem, wp_sem, wf_sem, wown_sem, fs_sem, fr_sem, os_sem, or_sem,
):
    f = lax.axis_index("frame")
    m = lax.axis_index("mp")
    clip8 = (f // 8) * 8
    j = f % 8
    cx = j // 2
    core = f % 2

    def mate(i):
        step = (1 + i % 3) * (1 - i // 6)
        return ((cx + step) % 4) * 2 + (core + i) % 2

    def source(i):
        step = (1 + i % 3) * (1 - i // 6)
        return ((cx + 4 - step) % 4) * 2 + (core + i) % 2

    def x_copy(i, slot):
        first = mate(i % 8) * 32 + (i // 8) * 16
        return pltpu.make_async_copy(x_ref.at[:, pl.ds(first, 16), :], xb.at[slot], xsem.at[slot])

    def w_in(n):
        ends = ((wt_hbm, wt_ref), (wout_hbm, wout_ref), (wllm_hbm, wllm_ref))[n]
        return pltpu.make_async_copy(*ends, in_sem.at[n])

    x_copy(0, 0).start()
    w_in(0).start()
    x_copy(1, 1).start()
    w_in(1).start()
    w_in(2).start()

    def xs_copy(half):
        return pltpu.make_async_copy(x_ref.at[:, pl.ds(m * 32 + half * 16, 16), :], xs.at[half], xssem.at[half])

    barrier = pltpu.get_barrier_semaphore()

    def greet(i, _):
        pl.semaphore_signal(barrier, inc=1, device_id=((f + i) % 16, m), device_id_type=MESH)
        return 0

    lax.fori_loop(1, 16, greet, 0)

    def greet_mp(i, _):
        pl.semaphore_signal(barrier, inc=1, device_id=(f, (m + i) % 8), device_id_type=MESH)
        return 0

    lax.fori_loop(1, 8, greet_mp, 0)

    def greet_back(i, _):
        @pl.when(jnp.logical_or(j != m, i != m))
        def _():
            pl.semaphore_signal(barrier, inc=1, device_id=(clip8 + m, i), device_id_type=MESH)

        return 0

    lax.fori_loop(0, 8, greet_back, 0)

    row, col = iota((128, 128), 0), iota((128, 128), 1)
    perm[...] = jnp.where((row >> 4 == (col & 7)) & ((row & 15) == col >> 3), 1.0, 0.0).astype(BF)
    row, col = iota((128, 512), 0), iota((128, 512), 1)
    hit = ((col >> 7) == ((row >> 2) & 3)) & (((col & 127) >> 2) == ((row >> 4) * 4 + (row & 3)))
    pool[...] = jnp.where(hit, 0.25, 0.0).astype(BF)
    tv[...] = jnp.where(iota((8, 128, 256), 2) == W, 1.0, 0.0).astype(BF)

    zh, y = m // 4, m % 4
    across = (m + 4) % 8

    def ring(k):
        return zh * 4 + (y + k) % 4

    def behind(k):
        return zh * 4 + (y + 4 - k) % 4

    def w_z():
        return pltpu.make_async_remote_copy(
            src_ref=wout_ref, dst_ref=wall.at[m], send_sem=ws_sem.at[0], recv_sem=wr_sem.at[0],
            device_id=(f, across), device_id_type=MESH,
        )

    def w_y(k):
        return pltpu.make_async_remote_copy(
            src_ref=wout_ref, dst_ref=wall.at[m], send_sem=ws_sem.at[k], recv_sem=wr_sem.at[k],
            device_id=(f, ring(k)), device_id_type=MESH,
        )

    def w_on(k):
        return pltpu.make_async_remote_copy(
            src_ref=wall.at[across], dst_ref=wall.at[across], send_sem=ws_sem.at[k], recv_sem=wr_sem.at[k],
            device_id=(f, ring(k)), device_id_type=MESH,
        )

    def w_pass(k, shard):
        return pltpu.make_async_remote_copy(
            src_ref=wall.at[shard], dst_ref=wall.at[shard], send_sem=wp_sem.at[k], recv_sem=wf_sem.at[k],
            device_id=(f + 1 - 2 * core, m), device_id_type=MESH,
        )

    def q_copy(i, half):
        to = mate(i % 8)
        chunk = (i // 8) * 2 + half
        return pltpu.make_async_remote_copy(
            src_ref=qsend.at[i, half], dst_ref=qrecv.at[chunk, j], send_sem=qs_sem.at[i, half],
            recv_sem=qr_sem.at[chunk, i % 8], device_id=(clip8 + to, m), device_id_type=MESH,
        )

    def q_own(i, half):
        chunk = (i // 8) * 2 + half
        return pltpu.make_async_copy(qsend.at[i, half], qrecv.at[chunk, j], qr_sem.at[chunk, 6])

    def q_start(i, half):
        @pl.when(i % 8 == 6)
        def _():
            q_own(i, half).start()

        @pl.when(i % 8 != 6)
        def _():
            q_copy(i, half).start()

    def normalize(slot, to):
        for n in range(8):
            v = norm_rows(xb[slot, 2 * n : 2 * n + 2].astype(F32).reshape(32, D), gain_ref[...].reshape(1, D))
            v = v.reshape(2, 2, 8, D)
            to[16 * n : 16 * n + 16, :] = v[:, 0].reshape(16, D).astype(BF)
            to[128 + 16 * n : 144 + 16 * n, :] = v[:, 1].reshape(16, D).astype(BF)

    def project(i, now, later, slot):
        @pl.when(i + 1 < 16)
        def _():
            x_copy(i + 1, slot).wait()

        qkv = lax.dot_general(wt_ref[...], now[...], NT, preferred_element_type=F32)
        qsend[i, 0] = qkv[:, :128].astype(BF)
        qsend[i, 1] = qkv[:, 128:].astype(BF)
        normalize(slot, later)

        @pl.when(i + 3 < 16)
        def _():
            x_copy(i + 3, slot).start()

    def two(n, _):
        project(2 * n, nb0, nb1, 1)
        project(2 * n + 1, nb1, nb0, 0)
        return 0

    def two_sent(n, _):
        two(n, 0)
        q_start(2 * n, 0)
        q_start(2 * n + 1, 0)
        return 0

    w_in(0).wait()
    x_copy(0, 0).wait()
    normalize(0, nb0)
    x_copy(2, 0).start()
    lax.fori_loop(0, 2, two, 0)
    w_in(1).wait()
    w_in(2).wait()

    @pl.when(j == m)
    def _():
        pl.semaphore_wait(barrier, 29)

    @pl.when(j != m)
    def _():
        pl.semaphore_wait(barrier, 30)

    def first(i, _):
        q_start(i, 0)
        return 0

    lax.fori_loop(0, 4, first, 0)

    @pl.when(core == 0)
    def _():
        for k in range(1, 4):
            w_y(k).start()

    @pl.when(core == 1)
    def _():
        w_z().start()

    def two_later(n, _):
        two(n, 0)
        q_start(2 * n - 8, 1)
        q_start(2 * n - 7, 1)
        return 0

    lax.fori_loop(2, 4, two_sent, 0)
    lax.fori_loop(4, 6, two_later, 0)

    @pl.when(core == 1)
    def _():
        w_z().wait()
        for k in range(1, 4):
            w_on(k).start()

    own_w = pltpu.make_async_copy(wout_ref, wall.at[m], wown_sem)
    own_w.start()
    for half in range(2):
        xs_copy(half).start()
    lax.fori_loop(6, 8, two_later, 0)

    def p_copy(chunk, i):
        to = (j + i) % 8
        rows = pl.ds(pl.multiple_of(chunk * 32, 32), 32)
        return pltpu.make_async_remote_copy(
            src_ref=psend.at[to, rows], dst_ref=arecv.at[m, rows], send_sem=ps_sem.at[chunk, i],
            recv_sem=pr_sem.at[chunk, m], device_id=(clip8 + to, j), device_id_type=MESH,
        )

    def p_own(chunk):
        rows = pl.ds(pl.multiple_of(chunk * 32, 32), 32)
        return pltpu.make_async_copy(psend.at[j, rows], arecv.at[m, rows], pr_sem.at[chunk, m])

    def attend(chunk, feed=None):
        def turn(i, _):
            pltpu.make_async_copy(qsend.at[0, 0], qrecv.at[chunk, source(i)], qr_sem.at[chunk, i]).wait()
            if feed is not None:
                q_start(8 + i, feed)
            s = source(i)
            block = qrecv.at[chunk, s]
            rows = pl.ds(pl.multiple_of(s * 16, 16), 16)
            for k, to in enumerate((tq, tk, tv)):
                part = lax.dot_general(perm[...], block[k * W : (k + 1) * W, :], NT, preferred_element_type=F32)
                to[:, rows, 0:W] = part.astype(BF).reshape(8, 16, W)
            return 0

        lax.fori_loop(0, 8, turn, 0)

        def quad(n, _):
            first = iota((128, W), 1) < HDIM
            wide = iota((128, 256), 1) < HDIM
            scale = math.log2(math.e) / math.sqrt(HDIM)
            for p in range(4):
                q = tq[4 * n + p]
                zero = jnp.zeros_like(q)
                q2 = jnp.concatenate([jnp.where(first, q, zero), jnp.where(first, zero, q)], axis=0)
                s = lax.dot_general(q2, tk[4 * n + p], NT, preferred_element_type=F32)
                top = jnp.max(s, axis=-1, keepdims=True)
                e = jnp.exp2((s - top) * scale).astype(BF)
                o = jnp.dot(e, tv[4 * n + p], preferred_element_type=F32)
                o = o * (1.0 / o[:, W : W + 1])
                att[p * 128 : (p + 1) * 128, :] = jnp.where(wide, o[:128], o[128:]).astype(BF)
            mean = jnp.dot(pool[...], att[...], preferred_element_type=F32).astype(BF)
            psend[:, pl.ds(pl.multiple_of(chunk * 32 + n * 16, 16), 16), :] = mean.reshape(8, 16, 256)
            return 0

        lax.fori_loop(0, 2, quad, 0)

        def back(i, _):
            here = jnp.logical_and(i == 0, j == m)

            @pl.when(here)
            def _():
                p_own(chunk).start()

            @pl.when(jnp.logical_not(here))
            def _():
                p_copy(chunk, i).start()

            return 0

        lax.fori_loop(0, 8, back, 0)

    def f_copy(chunk, e):
        owner = ring(2) if e == 5 else across if e > 3 else m
        rows = fin.at[owner, pl.ds(pl.multiple_of(chunk * 32, 32), 32)]
        return pltpu.make_async_remote_copy(
            src_ref=rows, dst_ref=rows, send_sem=fs_sem.at[chunk, e], recv_sem=fr_sem.at[chunk, e],
            device_id=(f, across if e in (0, 5) else ring((e - 1) % 3 + 1)), device_id_type=MESH,
        )

    def pass_on(chunk):
        f_copy(chunk, 0).wait_recv()
        f_copy(chunk, 4).start()
        f_copy(chunk, 6).start()
        f_copy(chunk, 2).wait_recv()
        f_copy(chunk, 5).start()

    def merge(chunk):
        rows = pl.ds(pl.multiple_of(chunk * 32, 32), 32)
        row, col = iota((32, 256), 0), iota((32, 256), 1)
        hit = ((col & 15) == (chunk % 2) * 8 + (row >> 2)) & ((col >> 6) == (row & 3))
        merged = jnp.dot(
            jnp.where(hit, 0.25, 0.0).astype(BF), xs[chunk // 2].reshape(256, D), preferred_element_type=F32
        )
        for s in range(8):
            pltpu.make_async_copy(psend.at[0, rows], arecv.at[s, rows], pr_sem.at[chunk, s]).wait()
        for s in range(8):
            merged += jnp.dot(arecv[s, rows, 0:W], wall[s], preferred_element_type=F32)
        fin[m, rows, :] = norm_rows(merged, pgain_ref[...].reshape(1, D)).astype(BF)

        for e in (0, 2, 1, 3):
            f_copy(chunk, e).start()

    def sort_rows():
        mine = slot_ref[pl.ds(pl.multiple_of(f * 8, 8), 8), :]
        parts = jnp.concatenate([mine >> 7, mine & 127], axis=0).astype(F32).astype(BF)
        lane, spot = iota((128, 1024), 0), iota((128, 1024), 1)
        patch = ((spot >> 5) & 3) * 32 + (spot >> 8) * 8 + ((spot >> 2) & 7)
        pick = jnp.where(patch == lane, 1.0, 0.0).astype(BF)
        picked = jnp.dot(parts, pick, preferred_element_type=F32)
        picked = picked[:8] * 128.0 + picked[8:]
        group, spot = iota((8, 1024), 0), iota((8, 1024), 1)
        keep = group == (spot & 3) * 2 + ((spot >> 7) & 1)
        along = jnp.sum(jnp.where(keep, picked, 0.0), axis=0, keepdims=True)
        same = jnp.where(iota((128, 128), 0) == iota((128, 128), 1), 1.0, 0.0).astype(BF)
        down = lax.dot_general(same, parts, NT, preferred_element_type=F32)
        down = down[:, :8] * 128.0 + down[:, 8:]
        count = jnp.zeros((128, 1024), F32)
        for n in range(8):
            count += jnp.where(down[:, n : n + 1] < along, 1.0, 0.0)
        rank = jnp.sum(count, axis=0, keepdims=True).astype(jnp.int32)

        def fill(n, _):
            rows = pl.ds(pl.multiple_of(n * 128, 128), 128)
            order[rows, :] = jnp.where(iota((128, 1024), 0) + n * 128 == rank, 1.0, 0.0).astype(BF)
            return 0

        lax.fori_loop(0, 8, fill, 0)

    def place_rows():
        def block(b, found):
            slots = slot_ref[pl.ds(pl.multiple_of(b * 8, 8), 8), :]
            high = (slots >> 7) - f * 8
            high = jnp.where((high >= 0) & (high < 8), high + b * 8, -1)
            low = slots & 127
            row = iota((128, 128), 0)
            highs = [jnp.where(high[n : n + 1] == row, 1.0, 0.0).astype(BF) for n in range(8)]
            lows = [jnp.where(low[n : n + 1] == row, 1.0, 0.0).astype(BF) for n in range(8)]
            return found + lax.dot_general(
                jnp.concatenate(lows, axis=1), jnp.concatenate(highs, axis=1), NT, preferred_element_type=F32
            )

        found = lax.fori_loop(0, 16, block, jnp.zeros((128, 128), F32))
        row, col = iota((128, 128), 0), iota((128, 128), 1)
        marks = found.astype(BF)
        before = jnp.where(row > col, 1.0, 0.0).astype(BF)
        rank = jnp.dot(before, marks, preferred_element_type=F32)
        sums = jnp.dot(jnp.ones((128, 128), BF), marks, preferred_element_type=F32).astype(BF)
        lower = jnp.where((row >> 3 == col >> 3) & (row < col), 1.0, 0.0).astype(BF)
        rank += jnp.dot(sums, lower, preferred_element_type=F32)
        key = found * (rank + ((col >> 3) * 64).astype(F32))
        for n in range(8):
            at = jnp.sum(jnp.where((col & 7) == n, key, 0.0), axis=1, keepdims=True).astype(jnp.int32)
            place[n * 128 : n * 128 + 128, :] = jnp.where(iota((128, 1024), 1) == at, 1.0, 0.0).astype(BF)

    sort_rows()
    place_rows()
    attend(0)

    own_w.wait()
    for half in range(2):
        xs_copy(half).wait()

    @pl.when(core == 0)
    def _():
        for k in range(1, 4):
            w_y(k).wait()
            w_pass(k, behind(k)).start()

    @pl.when(core == 1)
    def _():
        w_pass(0, across).start()
        for k in range(1, 4):
            w_on(k).wait()
            w_pass(k, (behind(k) + 4) % 8).start()

    attend(1, 0)

    @pl.when(core == 0)
    def _():
        for k in range(1, 4):
            w_pass(k, behind(k)).wait_send()
        w_pass(0, across).wait_recv()
        for k in range(1, 4):
            w_pass(k, (behind(k) + 4) % 8).wait_recv()

    @pl.when(core == 1)
    def _():
        w_pass(0, across).wait_send()
        for k in range(1, 4):
            w_pass(k, (behind(k) + 4) % 8).wait_send()
        for k in range(1, 4):
            w_pass(k, behind(k)).wait_recv()

    def read_out(chunk):
        f_rows = pl.ds(pl.multiple_of(chunk * 32, 32), 32)
        for e in (1, 3, 4, 5, 6):
            f_copy(chunk, e).wait_recv()
        rows = pl.ds(pl.multiple_of(chunk * 256, 256), 256)
        proj[rows, :] = jnp.dot(
            fin[:, f_rows, :].reshape(256, D), wllm_ref[...], preferred_element_type=F32
        ).astype(BF)

    merge(0)
    attend(2, 1)
    pass_on(0)
    merge(1)
    attend(3)
    merge(2)
    pass_on(1)
    merge(3)
    pass_on(2)
    read_out(0)
    pass_on(3)
    read_out(1)

    read_out(2)
    total[...] = jnp.dot(order[:, :768], proj[:768, :], preferred_element_type=F32)
    read_out(3)

    def o_copy(half, i):
        a, b, c = FAR[i]
        to = ((f // 8 + a) % 2) * 8 + ((cx + b) % 4) * 2 + (core + c) % 2
        return pltpu.make_async_remote_copy(
            src_ref=fsend.at[half, to], dst_ref=frecv.at[half, f], send_sem=os_sem.at[half, i],
            recv_sem=or_sem.at[half, i], device_id=(to, m), device_id_type=MESH,
        )

    for half in range(2):
        lanes = slice(half * 256, half * 256 + 256)
        turned = total[:, lanes] + jnp.dot(order[:, 768:], proj[768:, lanes], preferred_element_type=F32)
        fsend[half] = turned.astype(BF).reshape(16, 64, 256)
        for i in range(15):
            o_copy(half, i).start()
        frecv[half, f] = fsend[half, f]

    for half in range(2):
        for i in range(15):
            o_copy(half, i).wait_recv()
        out_ref[:, half * 256 : half * 256 + 256] = jnp.dot(
            place[...], frecv[half].reshape(1024, 256), preferred_element_type=F32
        ).astype(BF)

    def left_q(i, _):
        @pl.when(i % 8 != 6)
        def _():
            q_copy(i, 0).wait_send()
            q_copy(i, 1).wait_send()

        return 0

    lax.fori_loop(0, 16, left_q, 0)

    def left_p(i, _):
        @pl.when(jnp.logical_not(jnp.logical_and(i == 0, j == m)))
        def _():
            for chunk in range(CHUNKS):
                p_copy(chunk, i).wait_send()

        return 0

    lax.fori_loop(0, 8, left_p, 0)

    for chunk in range(CHUNKS):
        for e in range(7):
            f_copy(chunk, e).wait_send()
    for half in range(2):
        for i in range(15):
            o_copy(half, i).wait_send()


def per_device(stream, norm_gain, w_qkv, w_out, pool_gain, w_llm, owner_slot):
    frames = stream.reshape(16, 256, D)
    wt = jnp.swapaxes(w_qkv, 1, 2).reshape(3 * W, D)
    vmem, hbm = pl.BlockSpec(memory_space=pltpu.VMEM), pl.BlockSpec(memory_space=pl.ANY)
    dma = pltpu.SemaphoreType.DMA
    return pl.pallas_call(
        kernel,
        out_shape=jax.ShapeDtypeStruct((1024, 512), BF),
        in_specs=[hbm, vmem, hbm, hbm, vmem, hbm, vmem],
        out_specs=vmem,
        scratch_shapes=[
            pltpu.VMEM((3 * W, D), BF),
            pltpu.VMEM((W, D), BF),
            pltpu.VMEM((D, 512), BF),
            pltpu.VMEM((2, 16, 16, D), BF),
            pltpu.VMEM((256, D), BF),
            pltpu.VMEM((256, D), BF),
            pltpu.VMEM((16, 2, 3 * W, 128), BF),
            pltpu.VMEM((4, 8, 3 * W, 128), BF),
            pltpu.VMEM((8, 128, W), BF),
            pltpu.VMEM((8, 128, W), BF),
            pltpu.VMEM((8, 128, 256), BF),
            pltpu.VMEM((512, 256), BF),
            pltpu.VMEM((8, 128, 256), BF),
            pltpu.VMEM((8, 128, 256), BF),
            pltpu.VMEM((8, W, D), BF),
            pltpu.VMEM((2, 16, 16, D), BF),
            pltpu.VMEM((8, 128, D), BF),
            pltpu.VMEM((1024, 512), BF),
            pltpu.VMEM((1024, 512), F32),
            pltpu.VMEM((1024, 1024), BF),
            pltpu.VMEM((1024, 1024), BF),
            pltpu.VMEM((2, 16, 64, 256), BF),
            pltpu.VMEM((2, 16, 64, 256), BF),
            pltpu.VMEM((128, 128), BF),
            pltpu.VMEM((128, 512), BF),
            dma((3,)), dma((2,)), dma((2,)), dma((16, 2)), dma((4, 8)), dma((4, 8)), dma((4, 8)),
            dma((4,)), dma((4,)), dma((4,)), dma((4,)), dma, dma((4, 8)), dma((4, 8)), dma((2, 16)), dma((2, 16)),
        ],
        compiler_params=pltpu.CompilerParams(
            collective_id=0, has_side_effects=True, vmem_limit_bytes=56 * 2**20
        ),
        name="video_layer",
    )(frames, norm_gain, wt, w_out, pool_gain, w_llm, owner_slot.reshape(128, 128))


def solution(mesh):
    return jax.shard_map(
        per_device,
        mesh=mesh,
        in_specs=(
            P("frame", None), P(), P(None, None, "mp"), P("mp", None), P(), P(None, "mp"), P(),
        ),
        out_specs=P("frame", "mp"),
        check_vma=False,
    )
```

```python
import functools
import math

import jax
import jax.numpy as jnp
from jax import lax
from jax.experimental import pallas as pl
from jax.experimental.pallas import tpu as pltpu
from jax.sharding import PartitionSpec as P

MESH = pl.DeviceIdType.MESH
NT = (((1,), (1,)), ((), ()))
HDIM = 88
D = 1408
W = 176
EPS = 1e-6
CHUNKS = 4
FAR = sorted(((a, b, c) for a in (0, 1) for b in range(4) for c in (0, 1) if (a, b, c) != (0, 0, 0)), key=lambda s: -s[0] - min(s[1], 4 - s[1]))
BF = jnp.bfloat16
F32 = jnp.float32


def iota(shape, dim):
    return lax.broadcasted_iota(jnp.int32, shape, dim)


def norm_rows(values, gain):
    average = jnp.mean(values, axis=-1, keepdims=True)
    centered = values - average
    spread = jnp.mean(centered * centered, axis=-1, keepdims=True)
    return centered * lax.rsqrt(spread + EPS) * gain


def kernel(
    x_ref, gain_ref, wt_hbm, wout_hbm, pgain_ref, wllm_hbm, slot_ref, out_ref,
    wt_ref, wout_ref, wllm_ref, xb, nb0, nb1, qsend, qrecv, tq, tk, tv, att, psend, arecv, wall, xs, fin, proj, total, order, place, fsend, frecv, perm, pool,
    in_sem, xsem, xssem, qs_sem, qr_sem, ps_sem, pr_sem, ws_sem, wr_sem, wp_sem, wf_sem, wown_sem, fs_sem, fr_sem, os_sem, or_sem,
):
    f = lax.axis_index("frame")
    m = lax.axis_index("mp")
    clip8 = (f // 8) * 8
    j = f % 8
    cx = j // 2
    core = f % 2

    def mate(i):
        step = (1 + i % 3) * (1 - i // 6)
        return ((cx + step) % 4) * 2 + (core + i) % 2

    def source(i):
        step = (1 + i % 3) * (1 - i // 6)
        return ((cx + 4 - step) % 4) * 2 + (core + i) % 2

    def x_copy(i, slot):
        first = mate(i % 8) * 32 + (i // 8) * 16
        return pltpu.make_async_copy(x_ref.at[:, pl.ds(first, 16), :], xb.at[slot], xsem.at[slot])

    def w_in(n):
        ends = ((wt_hbm, wt_ref), (wout_hbm, wout_ref), (wllm_hbm, wllm_ref))[n]
        return pltpu.make_async_copy(*ends, in_sem.at[n])

    x_copy(0, 0).start()
    w_in(0).start()
    x_copy(1, 1).start()
    w_in(1).start()
    w_in(2).start()

    def xs_copy(half):
        return pltpu.make_async_copy(x_ref.at[:, pl.ds(m * 32 + half * 16, 16), :], xs.at[half], xssem.at[half])

    barrier = pltpu.get_barrier_semaphore()

    def greet(i, _):
        pl.semaphore_signal(barrier, inc=1, device_id=((f + i) % 16, m), device_id_type=MESH)
        return 0

    lax.fori_loop(1, 16, greet, 0)

    def greet_mp(i, _):
        pl.semaphore_signal(barrier, inc=1, device_id=(f, (m + i) % 8), device_id_type=MESH)
        return 0

    lax.fori_loop(1, 8, greet_mp, 0)

    def greet_back(i, _):
        @pl.when(jnp.logical_or(j != m, i != m))
        def _():
            pl.semaphore_signal(barrier, inc=1, device_id=(clip8 + m, i), device_id_type=MESH)

        return 0

    lax.fori_loop(0, 8, greet_back, 0)

    row, col = iota((128, 128), 0), iota((128, 128), 1)
    perm[...] = jnp.where((row >> 4 == (col & 7)) & ((row & 15) == col >> 3), 1.0, 0.0).astype(BF)
    row, col = iota((128, 512), 0), iota((128, 512), 1)
    hit = ((col >> 7) == ((row >> 2) & 3)) & (((col & 127) >> 2) == ((row >> 4) * 4 + (row & 3)))
    pool[...] = jnp.where(hit, 0.25, 0.0).astype(BF)
    tv[...] = jnp.where(iota((8, 128, 256), 2) == W, 1.0, 0.0).astype(BF)

    zh, y = m // 4, m % 4
    across = (m + 4) % 8

    def ring(k):
        return zh * 4 + (y + k) % 4

    def behind(k):
        return zh * 4 + (y + 4 - k) % 4

    def w_z():
        return pltpu.make_async_remote_copy(
            src_ref=wout_ref, dst_ref=wall.at[m], send_sem=ws_sem.at[0], recv_sem=wr_sem.at[0],
            device_id=(f, across), device_id_type=MESH,
        )

    def w_y(k):
        return pltpu.make_async_remote_copy(
            src_ref=wout_ref, dst_ref=wall.at[m], send_sem=ws_sem.at[k], recv_sem=wr_sem.at[k],
            device_id=(f, ring(k)), device_id_type=MESH,
        )

    def w_on(k):
        return pltpu.make_async_remote_copy(
            src_ref=wall.at[across], dst_ref=wall.at[across], send_sem=ws_sem.at[k], recv_sem=wr_sem.at[k],
            device_id=(f, ring(k)), device_id_type=MESH,
        )

    def w_pass(k, shard):
        return pltpu.make_async_remote_copy(
            src_ref=wall.at[shard], dst_ref=wall.at[shard], send_sem=wp_sem.at[k], recv_sem=wf_sem.at[k],
            device_id=(f + 1 - 2 * core, m), device_id_type=MESH,
        )

    def q_copy(i, half):
        to = mate(i % 8)
        chunk = (i // 8) * 2 + half
        return pltpu.make_async_remote_copy(
            src_ref=qsend.at[i, half], dst_ref=qrecv.at[chunk, j], send_sem=qs_sem.at[i, half],
            recv_sem=qr_sem.at[chunk, i % 8], device_id=(clip8 + to, m), device_id_type=MESH,
        )

    def q_own(i, half):
        chunk = (i // 8) * 2 + half
        return pltpu.make_async_copy(qsend.at[i, half], qrecv.at[chunk, j], qr_sem.at[chunk, 6])

    def q_start(i, half):
        @pl.when(i % 8 == 6)
        def _():
            q_own(i, half).start()

        @pl.when(i % 8 != 6)
        def _():
            q_copy(i, half).start()

    def normalize(slot, to):
        for n in range(8):
            v = norm_rows(xb[slot, 2 * n : 2 * n + 2].astype(F32).reshape(32, D), gain_ref[...].reshape(1, D))
            v = v.reshape(2, 2, 8, D)
            to[16 * n : 16 * n + 16, :] = v[:, 0].reshape(16, D).astype(BF)
            to[128 + 16 * n : 144 + 16 * n, :] = v[:, 1].reshape(16, D).astype(BF)

    def project(i, now, later, slot):
        @pl.when(i + 1 < 16)
        def _():
            x_copy(i + 1, slot).wait()

        qkv = lax.dot_general(wt_ref[...], now[...], NT, preferred_element_type=F32)
        qsend[i, 0] = qkv[:, :128].astype(BF)
        qsend[i, 1] = qkv[:, 128:].astype(BF)
        normalize(slot, later)

        @pl.when(i + 3 < 16)
        def _():
            x_copy(i + 3, slot).start()

    def two(n, _):
        project(2 * n, nb0, nb1, 1)
        project(2 * n + 1, nb1, nb0, 0)
        return 0

    def two_sent(n, _):
        two(n, 0)
        q_start(2 * n, 0)
        q_start(2 * n + 1, 0)
        return 0

    w_in(0).wait()
    x_copy(0, 0).wait()
    normalize(0, nb0)
    x_copy(2, 0).start()
    lax.fori_loop(0, 2, two, 0)
    w_in(1).wait()
    w_in(2).wait()

    @pl.when(j == m)
    def _():
        pl.semaphore_wait(barrier, 29)

    @pl.when(j != m)
    def _():
        pl.semaphore_wait(barrier, 30)

    def first(i, _):
        q_start(i, 0)
        return 0

    lax.fori_loop(0, 4, first, 0)

    @pl.when(core == 0)
    def _():
        for k in range(1, 4):
            w_y(k).start()

    @pl.when(core == 1)
    def _():
        w_z().start()

    def two_later(n, _):
        two(n, 0)
        q_start(2 * n - 8, 1)
        q_start(2 * n - 7, 1)
        return 0

    lax.fori_loop(2, 4, two_sent, 0)
    lax.fori_loop(4, 6, two_later, 0)

    @pl.when(core == 1)
    def _():
        w_z().wait()
        for k in range(1, 4):
            w_on(k).start()

    own_w = pltpu.make_async_copy(wout_ref, wall.at[m], wown_sem)
    own_w.start()
    for half in range(2):
        xs_copy(half).start()
    lax.fori_loop(6, 8, two_later, 0)

    def p_copy(chunk, i):
        to = (j + i) % 8
        rows = pl.ds(pl.multiple_of(chunk * 32, 32), 32)
        return pltpu.make_async_remote_copy(
            src_ref=psend.at[to, rows], dst_ref=arecv.at[m, rows], send_sem=ps_sem.at[chunk, i],
            recv_sem=pr_sem.at[chunk, m], device_id=(clip8 + to, j), device_id_type=MESH,
        )

    def p_own(chunk):
        rows = pl.ds(pl.multiple_of(chunk * 32, 32), 32)
        return pltpu.make_async_copy(psend.at[j, rows], arecv.at[m, rows], pr_sem.at[chunk, m])

    def attend(chunk, feed=None):
        def turn(i, _):
            pltpu.make_async_copy(qsend.at[0, 0], qrecv.at[chunk, source(i)], qr_sem.at[chunk, i]).wait()
            if feed is not None:
                q_start(8 + i, feed)
            s = source(i)
            block = qrecv.at[chunk, s]
            rows = pl.ds(pl.multiple_of(s * 16, 16), 16)
            for k, to in enumerate((tq, tk, tv)):
                part = lax.dot_general(perm[...], block[k * W : (k + 1) * W, :], NT, preferred_element_type=F32)
                to[:, rows, 0:W] = part.astype(BF).reshape(8, 16, W)
            return 0

        lax.fori_loop(0, 8, turn, 0)

        def quad(n, _):
            first = iota((128, W), 1) < HDIM
            wide = iota((128, 256), 1) < HDIM
            scale = math.log2(math.e) / math.sqrt(HDIM)
            for p in range(4):
                q = tq[4 * n + p]
                zero = jnp.zeros_like(q)
                q2 = jnp.concatenate([jnp.where(first, q, zero), jnp.where(first, zero, q)], axis=0)
                s = lax.dot_general(q2, tk[4 * n + p], NT, preferred_element_type=F32)
                top = jnp.max(s, axis=-1, keepdims=True)
                e = jnp.exp2((s - top) * scale).astype(BF)
                o = jnp.dot(e, tv[4 * n + p], preferred_element_type=F32)
                o = o * (1.0 / o[:, W : W + 1])
                att[p * 128 : (p + 1) * 128, :] = jnp.where(wide, o[:128], o[128:]).astype(BF)
            mean = jnp.dot(pool[...], att[...], preferred_element_type=F32).astype(BF)
            psend[:, pl.ds(pl.multiple_of(chunk * 32 + n * 16, 16), 16), :] = mean.reshape(8, 16, 256)
            return 0

        lax.fori_loop(0, 2, quad, 0)

        def back(i, _):
            here = jnp.logical_and(i == 0, j == m)

            @pl.when(here)
            def _():
                p_own(chunk).start()

            @pl.when(jnp.logical_not(here))
            def _():
                p_copy(chunk, i).start()

            return 0

        lax.fori_loop(0, 8, back, 0)

    def f_copy(chunk, e):
        owner = ring(2) if e == 5 else across if e > 3 else m
        rows = fin.at[owner, pl.ds(pl.multiple_of(chunk * 32, 32), 32)]
        return pltpu.make_async_remote_copy(
            src_ref=rows, dst_ref=rows, send_sem=fs_sem.at[chunk, e], recv_sem=fr_sem.at[chunk, e],
            device_id=(f, across if e in (0, 5) else ring((e - 1) % 3 + 1)), device_id_type=MESH,
        )

    def pass_on(chunk):
        f_copy(chunk, 0).wait_recv()
        f_copy(chunk, 4).start()
        f_copy(chunk, 6).start()
        f_copy(chunk, 2).wait_recv()
        f_copy(chunk, 5).start()

    def merge(chunk):
        rows = pl.ds(pl.multiple_of(chunk * 32, 32), 32)
        row, col = iota((32, 256), 0), iota((32, 256), 1)
        hit = ((col & 15) == (chunk % 2) * 8 + (row >> 2)) & ((col >> 6) == (row & 3))
        merged = jnp.dot(
            jnp.where(hit, 0.25, 0.0).astype(BF), xs[chunk // 2].reshape(256, D), preferred_element_type=F32
        )
        for s in range(8):
            pltpu.make_async_copy(psend.at[0, rows], arecv.at[s, rows], pr_sem.at[chunk, s]).wait()
        for s in range(8):
            merged += jnp.dot(arecv[s, rows, 0:W], wall[s], preferred_element_type=F32)
        fin[m, rows, :] = norm_rows(merged, pgain_ref[...].reshape(1, D)).astype(BF)

        for e in (0, 2, 1, 3):
            f_copy(chunk, e).start()

    def sort_rows():
        mine = slot_ref[pl.ds(pl.multiple_of(f * 8, 8), 8), :]
        parts = jnp.concatenate([mine >> 7, mine & 127], axis=0).astype(F32).astype(BF)
        lane, spot = iota((128, 1024), 0), iota((128, 1024), 1)
        patch = ((spot >> 5) & 3) * 32 + (spot >> 8) * 8 + ((spot >> 2) & 7)
        pick = jnp.where(patch == lane, 1.0, 0.0).astype(BF)
        picked = jnp.dot(parts, pick, preferred_element_type=F32)
        picked = picked[:8] * 128.0 + picked[8:]
        group, spot = iota((8, 1024), 0), iota((8, 1024), 1)
        keep = group == (spot & 3) * 2 + ((spot >> 7) & 1)
        along = jnp.sum(jnp.where(keep, picked, 0.0), axis=0, keepdims=True)
        same = jnp.where(iota((128, 128), 0) == iota((128, 128), 1), 1.0, 0.0).astype(BF)
        down = lax.dot_general(same, parts, NT, preferred_element_type=F32)
        down = down[:, :8] * 128.0 + down[:, 8:]
        count = jnp.zeros((128, 1024), F32)
        for n in range(8):
            count += jnp.where(down[:, n : n + 1] < along, 1.0, 0.0)
        rank = jnp.sum(count, axis=0, keepdims=True).astype(jnp.int32)

        def fill(n, _):
            rows = pl.ds(pl.multiple_of(n * 128, 128), 128)
            order[rows, :] = jnp.where(iota((128, 1024), 0) + n * 128 == rank, 1.0, 0.0).astype(BF)
            return 0

        lax.fori_loop(0, 8, fill, 0)

    def place_rows():
        def block(b, found):
            slots = slot_ref[pl.ds(pl.multiple_of(b * 8, 8), 8), :]
            high = (slots >> 7) - f * 8
            high = jnp.where((high >= 0) & (high < 8), high + b * 8, -1)
            low = slots & 127
            row = iota((128, 128), 0)
            highs = [jnp.where(high[n : n + 1] == row, 1.0, 0.0).astype(BF) for n in range(8)]
            lows = [jnp.where(low[n : n + 1] == row, 1.0, 0.0).astype(BF) for n in range(8)]
            return found + lax.dot_general(
                jnp.concatenate(lows, axis=1), jnp.concatenate(highs, axis=1), NT, preferred_element_type=F32
            )

        found = lax.fori_loop(0, 16, block, jnp.zeros((128, 128), F32))
        row, col = iota((128, 128), 0), iota((128, 128), 1)
        marks = found.astype(BF)
        before = jnp.where(row > col, 1.0, 0.0).astype(BF)
        rank = jnp.dot(before, marks, preferred_element_type=F32)
        sums = jnp.dot(jnp.ones((128, 128), BF), marks, preferred_element_type=F32).astype(BF)
        lower = jnp.where((row >> 3 == col >> 3) & (row < col), 1.0, 0.0).astype(BF)
        rank += jnp.dot(sums, lower, preferred_element_type=F32)
        key = found * (rank + ((col >> 3) * 64).astype(F32))
        for n in range(8):
            at = jnp.sum(jnp.where((col & 7) == n, key, 0.0), axis=1, keepdims=True).astype(jnp.int32)
            place[n * 128 : n * 128 + 128, :] = jnp.where(iota((128, 1024), 1) == at, 1.0, 0.0).astype(BF)

    attend(0)

    own_w.wait()
    for half in range(2):
        xs_copy(half).wait()

    @pl.when(core == 0)
    def _():
        for k in range(1, 4):
            w_y(k).wait()
            w_pass(k, behind(k)).start()

    @pl.when(core == 1)
    def _():
        w_pass(0, across).start()
        for k in range(1, 4):
            w_on(k).wait()
            w_pass(k, (behind(k) + 4) % 8).start()

    attend(1, 0)

    @pl.when(core == 0)
    def _():
        for k in range(1, 4):
            w_pass(k, behind(k)).wait_send()
        w_pass(0, across).wait_recv()
        for k in range(1, 4):
            w_pass(k, (behind(k) + 4) % 8).wait_recv()

    @pl.when(core == 1)
    def _():
        w_pass(0, across).wait_send()
        for k in range(1, 4):
            w_pass(k, (behind(k) + 4) % 8).wait_send()
        for k in range(1, 4):
            w_pass(k, behind(k)).wait_recv()

    def read_out(chunk):
        f_rows = pl.ds(pl.multiple_of(chunk * 32, 32), 32)
        for e in (1, 3, 4, 5, 6):
            f_copy(chunk, e).wait_recv()
        rows = pl.ds(pl.multiple_of(chunk * 256, 256), 256)
        proj[rows, :] = jnp.dot(
            fin[:, f_rows, :].reshape(256, D), wllm_ref[...], preferred_element_type=F32
        ).astype(BF)

    merge(0)
    attend(2, 1)
    pass_on(0)
    merge(1)
    sort_rows()
    place_rows()
    pass_on(1)
    attend(3)
    merge(2)
    pass_on(2)
    merge(3)
    read_out(0)
    read_out(1)
    pass_on(3)

    read_out(2)
    total[...] = jnp.dot(order[:, :768], proj[:768, :], preferred_element_type=F32)
    read_out(3)

    def o_copy(half, i):
        a, b, c = FAR[i]
        to = ((f // 8 + a) % 2) * 8 + ((cx + b) % 4) * 2 + (core + c) % 2
        return pltpu.make_async_remote_copy(
            src_ref=fsend.at[half, to], dst_ref=frecv.at[half, f], send_sem=os_sem.at[half, i],
            recv_sem=or_sem.at[half, i], device_id=(to, m), device_id_type=MESH,
        )

    for half in range(2):
        lanes = slice(half * 256, half * 256 + 256)
        turned = total[:, lanes] + jnp.dot(order[:, 768:], proj[768:, lanes], preferred_element_type=F32)
        fsend[half] = turned.astype(BF).reshape(16, 64, 256)
        for i in range(15):
            o_copy(half, i).start()
        frecv[half, f] = fsend[half, f]

    for half in range(2):
        for i in range(15):
            o_copy(half, i).wait_recv()
        out_ref[:, half * 256 : half * 256 + 256] = jnp.dot(
            place[...], frecv[half].reshape(1024, 256), preferred_element_type=F32
        ).astype(BF)

    def left_q(i, _):
        @pl.when(i % 8 != 6)
        def _():
            q_copy(i, 0).wait_send()
            q_copy(i, 1).wait_send()

        return 0

    lax.fori_loop(0, 16, left_q, 0)

    def left_p(i, _):
        @pl.when(jnp.logical_not(jnp.logical_and(i == 0, j == m)))
        def _():
            for chunk in range(CHUNKS):
                p_copy(chunk, i).wait_send()

        return 0

    lax.fori_loop(0, 8, left_p, 0)

    for chunk in range(CHUNKS):
        for e in range(7):
            f_copy(chunk, e).wait_send()
    for half in range(2):
        for i in range(15):
            o_copy(half, i).wait_send()


def per_device(stream, norm_gain, w_qkv, w_out, pool_gain, w_llm, owner_slot):
    frames = stream.reshape(16, 256, D)
    wt = jnp.swapaxes(w_qkv, 1, 2).reshape(3 * W, D)
    vmem, hbm = pl.BlockSpec(memory_space=pltpu.VMEM), pl.BlockSpec(memory_space=pl.ANY)
    dma = pltpu.SemaphoreType.DMA
    return pl.pallas_call(
        kernel,
        out_shape=jax.ShapeDtypeStruct((1024, 512), BF),
        in_specs=[hbm, vmem, hbm, hbm, vmem, hbm, vmem],
        out_specs=vmem,
        scratch_shapes=[
            pltpu.VMEM((3 * W, D), BF),
            pltpu.VMEM((W, D), BF),
            pltpu.VMEM((D, 512), BF),
            pltpu.VMEM((2, 16, 16, D), BF),
            pltpu.VMEM((256, D), BF),
            pltpu.VMEM((256, D), BF),
            pltpu.VMEM((16, 2, 3 * W, 128), BF),
            pltpu.VMEM((4, 8, 3 * W, 128), BF),
            pltpu.VMEM((8, 128, W), BF),
            pltpu.VMEM((8, 128, W), BF),
            pltpu.VMEM((8, 128, 256), BF),
            pltpu.VMEM((512, 256), BF),
            pltpu.VMEM((8, 128, 256), BF),
            pltpu.VMEM((8, 128, 256), BF),
            pltpu.VMEM((8, W, D), BF),
            pltpu.VMEM((2, 16, 16, D), BF),
            pltpu.VMEM((8, 128, D), BF),
            pltpu.VMEM((1024, 512), BF),
            pltpu.VMEM((1024, 512), F32),
            pltpu.VMEM((1024, 1024), BF),
            pltpu.VMEM((1024, 1024), BF),
            pltpu.VMEM((2, 16, 64, 256), BF),
            pltpu.VMEM((2, 16, 64, 256), BF),
            pltpu.VMEM((128, 128), BF),
            pltpu.VMEM((128, 512), BF),
            dma((3,)), dma((2,)), dma((2,)), dma((16, 2)), dma((4, 8)), dma((4, 8)), dma((4, 8)),
            dma((4,)), dma((4,)), dma((4,)), dma((4,)), dma, dma((4, 8)), dma((4, 8)), dma((2, 16)), dma((2, 16)),
        ],
        compiler_params=pltpu.CompilerParams(
            collective_id=0, has_side_effects=True, vmem_limit_bytes=56 * 2**20
        ),
        name="video_layer",
    )(frames, norm_gain, wt, w_out, pool_gain, w_llm, owner_slot.reshape(128, 128))


def solution(mesh):
    return jax.shard_map(
        per_device,
        mesh=mesh,
        in_specs=(
            P("frame", None), P(), P(None, None, "mp"), P("mp", None), P(), P(None, "mp"), P(),
        ),
        out_specs=P("frame", "mp"),
        check_vma=False,
    )
```

```python
import functools
import math

import jax
import jax.numpy as jnp
from jax import lax
from jax.experimental import pallas as pl
from jax.experimental.pallas import tpu as pltpu
from jax.sharding import PartitionSpec as P

MESH = pl.DeviceIdType.MESH
NT = (((1,), (1,)), ((), ()))
HDIM = 88
D = 1408
W = 176
EPS = 1e-6
CHUNKS = 4
FAR = sorted(((a, b, c) for a in (0, 1) for b in range(4) for c in (0, 1) if (a, b, c) != (0, 0, 0)), key=lambda s: -s[0] - min(s[1], 4 - s[1]))
BF = jnp.bfloat16
F32 = jnp.float32


def iota(shape, dim):
    return lax.broadcasted_iota(jnp.int32, shape, dim)


def norm_rows(values, gain):
    average = jnp.mean(values, axis=-1, keepdims=True)
    centered = values - average
    spread = jnp.mean(centered * centered, axis=-1, keepdims=True)
    return centered * lax.rsqrt(spread + EPS) * gain


def kernel(
    x_ref, gain_ref, wt_hbm, wout_hbm, pgain_ref, wllm_hbm, slot_ref, out_ref,
    wt_ref, wout_ref, wllm_ref, xb, nb0, nb1, qsend, qrecv, tq, tk, tv, att, psend, arecv, wall, xs, fin, proj, total, order, place, fsend, frecv, perm, pool,
    in_sem, xsem, xssem, qs_sem, qr_sem, ps_sem, pr_sem, ws_sem, wr_sem, wp_sem, wf_sem, wown_sem, fs_sem, fr_sem, os_sem, or_sem,
):
    f = lax.axis_index("frame")
    m = lax.axis_index("mp")
    clip8 = (f // 8) * 8
    j = f % 8
    cx = j // 2
    core = f % 2

    def mate(i):
        step = (1 + i % 3) * (1 - i // 6)
        return ((cx + step) % 4) * 2 + (core + i) % 2

    def source(i):
        step = (1 + i % 3) * (1 - i // 6)
        return ((cx + 4 - step) % 4) * 2 + (core + i) % 2

    def x_copy(i, slot):
        first = mate(i % 8) * 32 + (i // 8) * 16
        return pltpu.make_async_copy(x_ref.at[:, pl.ds(first, 16), :], xb.at[slot], xsem.at[slot])

    def w_in(n):
        ends = ((wt_hbm, wt_ref), (wout_hbm, wout_ref), (wllm_hbm, wllm_ref))[n]
        return pltpu.make_async_copy(*ends, in_sem.at[n])

    x_copy(0, 0).start()
    w_in(0).start()
    x_copy(1, 1).start()
    w_in(1).start()
    w_in(2).start()

    def xs_copy(half):
        return pltpu.make_async_copy(x_ref.at[:, pl.ds(m * 32 + half * 16, 16), :], xs.at[half], xssem.at[half])

    barrier = pltpu.get_barrier_semaphore()

    def greet(i, _):
        pl.semaphore_signal(barrier, inc=1, device_id=((f + i) % 16, m), device_id_type=MESH)
        return 0

    lax.fori_loop(1, 16, greet, 0)

    def greet_mp(i, _):
        pl.semaphore_signal(barrier, inc=1, device_id=(f, (m + i) % 8), device_id_type=MESH)
        return 0

    lax.fori_loop(1, 8, greet_mp, 0)

    def greet_back(i, _):
        @pl.when(jnp.logical_or(j != m, i != m))
        def _():
            pl.semaphore_signal(barrier, inc=1, device_id=(clip8 + m, i), device_id_type=MESH)

        return 0

    lax.fori_loop(0, 8, greet_back, 0)

    row, col = iota((128, 128), 0), iota((128, 128), 1)
    perm[...] = jnp.where((row >> 4 == (col & 7)) & ((row & 15) == col >> 3), 1.0, 0.0).astype(BF)
    row, col = iota((128, 512), 0), iota((128, 512), 1)
    hit = ((col >> 7) == ((row >> 2) & 3)) & (((col & 127) >> 2) == ((row >> 4) * 4 + (row & 3)))
    pool[...] = jnp.where(hit, 0.25, 0.0).astype(BF)
    tv[...] = jnp.where(iota((8, 128, 256), 2) == W, 1.0, 0.0).astype(BF)

    zh, y = m // 4, m % 4
    across = (m + 4) % 8

    def ring(k):
        return zh * 4 + (y + k) % 4

    def behind(k):
        return zh * 4 + (y + 4 - k) % 4

    def w_z():
        return pltpu.make_async_remote_copy(
            src_ref=wout_ref, dst_ref=wall.at[m], send_sem=ws_sem.at[0], recv_sem=wr_sem.at[0],
            device_id=(f, across), device_id_type=MESH,
        )

    def w_y(k):
        return pltpu.make_async_remote_copy(
            src_ref=wout_ref, dst_ref=wall.at[m], send_sem=ws_sem.at[k], recv_sem=wr_sem.at[k],
            device_id=(f, ring(k)), device_id_type=MESH,
        )

    def w_on(k):
        return pltpu.make_async_remote_copy(
            src_ref=wall.at[across], dst_ref=wall.at[across], send_sem=ws_sem.at[k], recv_sem=wr_sem.at[k],
            device_id=(f, ring(k)), device_id_type=MESH,
        )

    def w_pass(k, shard):
        return pltpu.make_async_remote_copy(
            src_ref=wall.at[shard], dst_ref=wall.at[shard], send_sem=wp_sem.at[k], recv_sem=wf_sem.at[k],
            device_id=(f + 1 - 2 * core, m), device_id_type=MESH,
        )

    def q_copy(i, half):
        to = mate(i % 8)
        chunk = (i // 8) * 2 + half
        return pltpu.make_async_remote_copy(
            src_ref=qsend.at[i, half], dst_ref=qrecv.at[chunk, j], send_sem=qs_sem.at[i, half],
            recv_sem=qr_sem.at[chunk, i % 8], device_id=(clip8 + to, m), device_id_type=MESH,
        )

    def q_own(i, half):
        chunk = (i // 8) * 2 + half
        return pltpu.make_async_copy(qsend.at[i, half], qrecv.at[chunk, j], qr_sem.at[chunk, 6])

    def q_start(i, half):
        @pl.when(i % 8 == 6)
        def _():
            q_own(i, half).start()

        @pl.when(i % 8 != 6)
        def _():
            q_copy(i, half).start()

    def normalize(slot, to):
        for n in range(8):
            v = norm_rows(xb[slot, 2 * n : 2 * n + 2].astype(F32).reshape(32, D), gain_ref[...].reshape(1, D))
            v = v.reshape(2, 2, 8, D)
            to[16 * n : 16 * n + 16, :] = v[:, 0].reshape(16, D).astype(BF)
            to[128 + 16 * n : 144 + 16 * n, :] = v[:, 1].reshape(16, D).astype(BF)

    def project(i, now, later, slot):
        @pl.when(i + 1 < 16)
        def _():
            x_copy(i + 1, slot).wait()

        qkv = lax.dot_general(wt_ref[...], now[...], NT, preferred_element_type=F32)
        qsend[i, 0] = qkv[:, :128].astype(BF)
        qsend[i, 1] = qkv[:, 128:].astype(BF)
        normalize(slot, later)

        @pl.when(i + 3 < 16)
        def _():
            x_copy(i + 3, slot).start()

    def two(n, _):
        project(2 * n, nb0, nb1, 1)
        project(2 * n + 1, nb1, nb0, 0)
        return 0

    def two_sent(n, _):
        two(n, 0)
        q_start(2 * n, 0)
        q_start(2 * n + 1, 0)
        return 0

    w_in(0).wait()
    x_copy(0, 0).wait()
    normalize(0, nb0)
    x_copy(2, 0).start()
    lax.fori_loop(0, 2, two, 0)
    w_in(1).wait()
    w_in(2).wait()

    @pl.when(j == m)
    def _():
        pl.semaphore_wait(barrier, 29)

    @pl.when(j != m)
    def _():
        pl.semaphore_wait(barrier, 30)

    def first(i, _):
        q_start(i, 0)
        return 0

    lax.fori_loop(0, 4, first, 0)

    @pl.when(core == 0)
    def _():
        for k in range(1, 4):
            w_y(k).start()

    @pl.when(core == 1)
    def _():
        w_z().start()

    def two_later(n, _):
        two(n, 0)
        q_start(2 * n - 8, 1)
        q_start(2 * n - 7, 1)
        return 0

    lax.fori_loop(2, 4, two_sent, 0)
    lax.fori_loop(4, 6, two_later, 0)

    @pl.when(core == 1)
    def _():
        w_z().wait()
        for k in range(1, 4):
            w_on(k).start()

    own_w = pltpu.make_async_copy(wout_ref, wall.at[m], wown_sem)
    own_w.start()
    for half in range(2):
        xs_copy(half).start()
    lax.fori_loop(6, 8, two_later, 0)

    def p_copy(chunk, i):
        to = (j + i) % 8
        rows = pl.ds(pl.multiple_of(chunk * 32, 32), 32)
        return pltpu.make_async_remote_copy(
            src_ref=psend.at[to, rows], dst_ref=arecv.at[m, rows], send_sem=ps_sem.at[chunk, i],
            recv_sem=pr_sem.at[chunk, m], device_id=(clip8 + to, j), device_id_type=MESH,
        )

    def p_own(chunk):
        rows = pl.ds(pl.multiple_of(chunk * 32, 32), 32)
        return pltpu.make_async_copy(psend.at[j, rows], arecv.at[m, rows], pr_sem.at[chunk, m])

    def attend(chunk, feed=None):
        def turn(i, _):
            pltpu.make_async_copy(qsend.at[0, 0], qrecv.at[chunk, source(i)], qr_sem.at[chunk, i]).wait()
            if feed is not None:
                q_start(8 + i, feed)
            s = source(i)
            block = qrecv.at[chunk, s]
            rows = pl.ds(pl.multiple_of(s * 16, 16), 16)
            for k, to in enumerate((tq, tk, tv)):
                part = lax.dot_general(perm[...], block[k * W : (k + 1) * W, :], NT, preferred_element_type=F32)
                to[:, rows, 0:W] = part.astype(BF).reshape(8, 16, W)
            return 0

        lax.fori_loop(0, 8, turn, 0)

        def quad(n, _):
            first = iota((128, W), 1) < HDIM
            wide = iota((128, 256), 1) < HDIM
            scale = math.log2(math.e) / math.sqrt(HDIM)
            for p in range(4):
                q = tq[4 * n + p]
                zero = jnp.zeros_like(q)
                q2 = jnp.concatenate([jnp.where(first, q, zero), jnp.where(first, zero, q)], axis=0)
                s = lax.dot_general(q2, tk[4 * n + p], NT, preferred_element_type=F32)
                top = jnp.max(s, axis=-1, keepdims=True)
                e = jnp.exp2((s - top) * scale).astype(BF)
                o = jnp.dot(e, tv[4 * n + p], preferred_element_type=F32)
                o = o * (1.0 / o[:, W : W + 1])
                att[p * 128 : (p + 1) * 128, :] = jnp.where(wide, o[:128], o[128:]).astype(BF)
            mean = jnp.dot(pool[...], att[...], preferred_element_type=F32).astype(BF)
            psend[:, pl.ds(pl.multiple_of(chunk * 32 + n * 16, 16), 16), :] = mean.reshape(8, 16, 256)
            return 0

        lax.fori_loop(0, 2, quad, 0)

        def back(i, _):
            here = jnp.logical_and(i == 0, j == m)

            @pl.when(here)
            def _():
                p_own(chunk).start()

            @pl.when(jnp.logical_not(here))
            def _():
                p_copy(chunk, i).start()

            return 0

        lax.fori_loop(0, 8, back, 0)

    def f_copy(chunk, e):
        owner = ring(2) if e == 5 else across if e > 3 else m
        rows = fin.at[owner, pl.ds(pl.multiple_of(chunk * 32, 32), 32)]
        return pltpu.make_async_remote_copy(
            src_ref=rows, dst_ref=rows, send_sem=fs_sem.at[chunk, e], recv_sem=fr_sem.at[chunk, e],
            device_id=(f, across if e in (0, 5) else ring((e - 1) % 3 + 1)), device_id_type=MESH,
        )

    def pass_on(chunk):
        f_copy(chunk, 0).wait_recv()
        f_copy(chunk, 4).start()
        f_copy(chunk, 6).start()
        f_copy(chunk, 2).wait_recv()
        f_copy(chunk, 5).start()

    def merge(chunk):
        rows = pl.ds(pl.multiple_of(chunk * 32, 32), 32)
        row, col = iota((32, 256), 0), iota((32, 256), 1)
        hit = ((col & 15) == (chunk % 2) * 8 + (row >> 2)) & ((col >> 6) == (row & 3))
        merged = jnp.dot(
            jnp.where(hit, 0.25, 0.0).astype(BF), xs[chunk // 2].reshape(256, D), preferred_element_type=F32
        )
        for s in range(8):
            pltpu.make_async_copy(psend.at[0, rows], arecv.at[s, rows], pr_sem.at[chunk, s]).wait()
        for s in range(8):
            merged += jnp.dot(arecv[s, rows, 0:W], wall[s], preferred_element_type=F32)
        fin[m, rows, :] = norm_rows(merged, pgain_ref[...].reshape(1, D)).astype(BF)

        for e in (0, 2, 1, 3):
            f_copy(chunk, e).start()

    def sort_rows():
        mine = slot_ref[pl.ds(pl.multiple_of(f * 8, 8), 8), :]
        parts = jnp.concatenate([mine >> 7, mine & 127], axis=0).astype(F32).astype(BF)
        lane, spot = iota((128, 1024), 0), iota((128, 1024), 1)
        patch = ((spot >> 5) & 3) * 32 + (spot >> 8) * 8 + ((spot >> 2) & 7)
        pick = jnp.where(patch == lane, 1.0, 0.0).astype(BF)
        picked = jnp.dot(parts, pick, preferred_element_type=F32)
        picked = picked[:8] * 128.0 + picked[8:]
        group, spot = iota((8, 1024), 0), iota((8, 1024), 1)
        keep = group == (spot & 3) * 2 + ((spot >> 7) & 1)
        along = jnp.sum(jnp.where(keep, picked, 0.0), axis=0, keepdims=True)
        same = jnp.where(iota((128, 128), 0) == iota((128, 128), 1), 1.0, 0.0).astype(BF)
        down = lax.dot_general(same, parts, NT, preferred_element_type=F32)
        down = down[:, :8] * 128.0 + down[:, 8:]
        count = jnp.zeros((128, 1024), F32)
        for n in range(8):
            count += jnp.where(down[:, n : n + 1] < along, 1.0, 0.0)
        rank = jnp.sum(count, axis=0, keepdims=True).astype(jnp.int32)

        def fill(n, _):
            rows = pl.ds(pl.multiple_of(n * 128, 128), 128)
            order[rows, :] = jnp.where(iota((128, 1024), 0) + n * 128 == rank, 1.0, 0.0).astype(BF)
            return 0

        lax.fori_loop(0, 8, fill, 0)

    def place_rows():
        def block(b, found):
            slots = slot_ref[pl.ds(pl.multiple_of(b * 8, 8), 8), :]
            high = (slots >> 7) - f * 8
            high = jnp.where((high >= 0) & (high < 8), high + b * 8, -1)
            low = slots & 127
            row = iota((128, 128), 0)
            highs = [jnp.where(high[n : n + 1] == row, 1.0, 0.0).astype(BF) for n in range(8)]
            lows = [jnp.where(low[n : n + 1] == row, 1.0, 0.0).astype(BF) for n in range(8)]
            return found + lax.dot_general(
                jnp.concatenate(lows, axis=1), jnp.concatenate(highs, axis=1), NT, preferred_element_type=F32
            )

        found = lax.fori_loop(0, 16, block, jnp.zeros((128, 128), F32))
        row, col = iota((128, 128), 0), iota((128, 128), 1)
        marks = found.astype(BF)
        before = jnp.where(row > col, 1.0, 0.0).astype(BF)
        rank = jnp.dot(before, marks, preferred_element_type=F32)
        sums = jnp.dot(jnp.ones((128, 128), BF), marks, preferred_element_type=F32).astype(BF)
        lower = jnp.where((row >> 3 == col >> 3) & (row < col), 1.0, 0.0).astype(BF)
        rank += jnp.dot(sums, lower, preferred_element_type=F32)
        key = found * (rank + ((col >> 3) * 64).astype(F32))
        for n in range(8):
            at = jnp.sum(jnp.where((col & 7) == n, key, 0.0), axis=1, keepdims=True).astype(jnp.int32)
            place[n * 128 : n * 128 + 128, :] = jnp.where(iota((128, 1024), 1) == at, 1.0, 0.0).astype(BF)

    attend(0)

    own_w.wait()
    for half in range(2):
        xs_copy(half).wait()

    @pl.when(core == 0)
    def _():
        for k in range(1, 4):
            w_y(k).wait()
            w_pass(k, behind(k)).start()

    @pl.when(core == 1)
    def _():
        w_pass(0, across).start()
        for k in range(1, 4):
            w_on(k).wait()
            w_pass(k, (behind(k) + 4) % 8).start()

    attend(1, 0)

    @pl.when(core == 0)
    def _():
        for k in range(1, 4):
            w_pass(k, behind(k)).wait_send()
        w_pass(0, across).wait_recv()
        for k in range(1, 4):
            w_pass(k, (behind(k) + 4) % 8).wait_recv()

    @pl.when(core == 1)
    def _():
        w_pass(0, across).wait_send()
        for k in range(1, 4):
            w_pass(k, (behind(k) + 4) % 8).wait_send()
        for k in range(1, 4):
            w_pass(k, behind(k)).wait_recv()

    def read_out(chunk):
        f_rows = pl.ds(pl.multiple_of(chunk * 32, 32), 32)
        for e in (1, 3, 4, 5, 6):
            f_copy(chunk, e).wait_recv()
        rows = pl.ds(pl.multiple_of(chunk * 256, 256), 256)
        proj[rows, :] = jnp.dot(
            fin[:, f_rows, :].reshape(256, D), wllm_ref[...], preferred_element_type=F32
        ).astype(BF)

    merge(0)
    attend(2, 1)
    pass_on(0)
    merge(1)
    sort_rows()
    place_rows()
    attend(3)
    pass_on(1)
    merge(2)
    pass_on(2)
    merge(3)
    read_out(0)
    read_out(1)
    pass_on(3)

    read_out(2)
    total[...] = jnp.dot(order[:, :768], proj[:768, :], preferred_element_type=F32)
    read_out(3)

    def o_copy(half, i):
        a, b, c = FAR[i]
        to = ((f // 8 + a) % 2) * 8 + ((cx + b) % 4) * 2 + (core + c) % 2
        return pltpu.make_async_remote_copy(
            src_ref=fsend.at[half, to], dst_ref=frecv.at[half, f], send_sem=os_sem.at[half, i],
            recv_sem=or_sem.at[half, i], device_id=(to, m), device_id_type=MESH,
        )

    for half in range(2):
        lanes = slice(half * 256, half * 256 + 256)
        turned = total[:, lanes] + jnp.dot(order[:, 768:], proj[768:, lanes], preferred_element_type=F32)
        fsend[half] = turned.astype(BF).reshape(16, 64, 256)
        for i in range(15):
            o_copy(half, i).start()
        frecv[half, f] = fsend[half, f]

    for half in range(2):
        for i in range(15):
            o_copy(half, i).wait_recv()
        out_ref[:, half * 256 : half * 256 + 256] = jnp.dot(
            place[...], frecv[half].reshape(1024, 256), preferred_element_type=F32
        ).astype(BF)

    def left_q(i, _):
        @pl.when(i % 8 != 6)
        def _():
            q_copy(i, 0).wait_send()
            q_copy(i, 1).wait_send()

        return 0

    lax.fori_loop(0, 16, left_q, 0)

    def left_p(i, _):
        @pl.when(jnp.logical_not(jnp.logical_and(i == 0, j == m)))
        def _():
            for chunk in range(CHUNKS):
                p_copy(chunk, i).wait_send()

        return 0

    lax.fori_loop(0, 8, left_p, 0)

    for chunk in range(CHUNKS):
        for e in range(7):
            f_copy(chunk, e).wait_send()
    for half in range(2):
        for i in range(15):
            o_copy(half, i).wait_send()


def per_device(stream, norm_gain, w_qkv, w_out, pool_gain, w_llm, owner_slot):
    frames = stream.reshape(16, 256, D)
    wt = jnp.swapaxes(w_qkv, 1, 2).reshape(3 * W, D)
    vmem, hbm = pl.BlockSpec(memory_space=pltpu.VMEM), pl.BlockSpec(memory_space=pl.ANY)
    dma = pltpu.SemaphoreType.DMA
    return pl.pallas_call(
        kernel,
        out_shape=jax.ShapeDtypeStruct((1024, 512), BF),
        in_specs=[hbm, vmem, hbm, hbm, vmem, hbm, vmem],
        out_specs=vmem,
        scratch_shapes=[
            pltpu.VMEM((3 * W, D), BF),
            pltpu.VMEM((W, D), BF),
            pltpu.VMEM((D, 512), BF),
            pltpu.VMEM((2, 16, 16, D), BF),
            pltpu.VMEM((256, D), BF),
            pltpu.VMEM((256, D), BF),
            pltpu.VMEM((16, 2, 3 * W, 128), BF),
            pltpu.VMEM((4, 8, 3 * W, 128), BF),
            pltpu.VMEM((8, 128, W), BF),
            pltpu.VMEM((8, 128, W), BF),
            pltpu.VMEM((8, 128, 256), BF),
            pltpu.VMEM((512, 256), BF),
            pltpu.VMEM((8, 128, 256), BF),
            pltpu.VMEM((8, 128, 256), BF),
            pltpu.VMEM((8, W, D), BF),
            pltpu.VMEM((2, 16, 16, D), BF),
            pltpu.VMEM((8, 128, D), BF),
            pltpu.VMEM((1024, 512), BF),
            pltpu.VMEM((1024, 512), F32),
            pltpu.VMEM((1024, 1024), BF),
            pltpu.VMEM((1024, 1024), BF),
            pltpu.VMEM((2, 16, 64, 256), BF),
            pltpu.VMEM((2, 16, 64, 256), BF),
            pltpu.VMEM((128, 128), BF),
            pltpu.VMEM((128, 512), BF),
            dma((3,)), dma((2,)), dma((2,)), dma((16, 2)), dma((4, 8)), dma((4, 8)), dma((4, 8)),
            dma((4,)), dma((4,)), dma((4,)), dma((4,)), dma, dma((4, 8)), dma((4, 8)), dma((2, 16)), dma((2, 16)),
        ],
        compiler_params=pltpu.CompilerParams(
            collective_id=0, has_side_effects=True, vmem_limit_bytes=56 * 2**20
        ),
        name="video_layer",
    )(frames, norm_gain, wt, w_out, pool_gain, w_llm, owner_slot.reshape(128, 128))


def solution(mesh):
    return jax.shard_map(
        per_device,
        mesh=mesh,
        in_specs=(
            P("frame", None), P(), P(None, None, "mp"), P("mp", None), P(), P(None, "mp"), P(),
        ),
        out_specs=P("frame", "mp"),
        check_vma=False,
    )
```
